128 devices in a mesh: dp: 16 (over x, y_lo, core), tensor: 8 (over z, y_hi).
Axes of the slice: x: 4, y: 4 (y_hi: 2, y_lo: 2; y = y_hi * 2 + y_lo), z: 4, core: 2. Of those that a mesh axis runs over, the one named last changes fastest.
Arguments:
- tokens: bfloat16 [8192, 2048], P('dp'), may hold values from -6 to 6
- cotangent: bfloat16 [8192, 2048], P('dp'), may hold values from -6 to 6
- group_sizes: int32 [16], P('dp'), may hold values from 4 to 16
- prefix_lens: int32 [16], P('dp'), may hold values from 64 to 128, as said below
- solution_lens: int32 [16, 16], P('dp'), may hold values from 1 to 445, as said below
- w_qkv: float32 [3, 2048, 2048], P(None, 'dp', 'tensor'), may hold values from -0.125 to 0.125
- w_out: float32 [2048, 2048], P('tensor', 'dp'), may hold values from -1 to 1
- w_up: float32 [2048, 8192], P('dp', 'tensor'), may hold values from -0.125 to 0.125
- w_down: float32 [8192, 2048], P('tensor', 'dp'), may hold values from -0.25 to 0.25
- norms: float32 [4, 2048], P(None, 'dp'), may hold values from -0.9 to 1.5, as said below
- first_qkv: float32 [3, 2048, 2048], P(None, 'dp', 'tensor'), as said below
- second_qkv: float32 [3, 2048, 2048], P(None, 'dp', 'tensor'), as said below
- first_out: float32 [2048, 2048], P('tensor', 'dp'), as said below
- second_out: float32 [2048, 2048], P('tensor', 'dp'), as said below
- first_up: float32 [2048, 8192], P('dp', 'tensor'), as said below
- second_up: float32 [2048, 8192], P('dp', 'tensor'), as said below
- first_down: float32 [8192, 2048], P('tensor', 'dp'), as said below
- second_down: float32 [8192, 2048], P('tensor', 'dp'), as said below
- first_norms: float32 [4, 2048], P(None, 'dp'), as said below
- second_norms: float32 [4, 2048], P(None, 'dp'), as said below
Outputs:
- block_out: bfloat16 [8192, 2048], P('dp')
- input_grad: float32 [8192, 2048], P('dp')
- grad_w_qkv: float32 [3, 2048, 2048], P(None, 'dp', 'tensor')
- new_first_qkv: float32 [3, 2048, 2048], P(None, 'dp', 'tensor')
- new_second_qkv: float32 [3, 2048, 2048], P(None, 'dp', 'tensor')
- new_w_qkv: float32 [3, 2048, 2048], P(None, 'dp', 'tensor')
- copy_w_qkv: bfloat16 [3, 2048, 2048], P(None, 'dp', 'tensor')
- grad_w_out: float32 [2048, 2048], P('tensor', 'dp')
- new_first_out: float32 [2048, 2048], P('tensor', 'dp')
- new_second_out: float32 [2048, 2048], P('tensor', 'dp')
- new_w_out: float32 [2048, 2048], P('tensor', 'dp')
- copy_w_out: bfloat16 [2048, 2048], P('tensor', 'dp')
- grad_w_up: float32 [2048, 8192], P('dp', 'tensor')
- new_first_up: float32 [2048, 8192], P('dp', 'tensor')
- new_second_up: float32 [2048, 8192], P('dp', 'tensor')
- new_w_up: float32 [2048, 8192], P('dp', 'tensor')
- copy_w_up: bfloat16 [2048, 8192], P('dp', 'tensor')
- grad_w_down: float32 [8192, 2048], P('tensor', 'dp')
- new_first_down: float32 [8192, 2048], P('tensor', 'dp')
- new_second_down: float32 [8192, 2048], P('tensor', 'dp')
- new_w_down: float32 [8192, 2048], P('tensor', 'dp')
- copy_w_down: bfloat16 [8192, 2048], P('tensor', 'dp')
- grad_norms: float32 [4, 2048], P(None, 'dp')
- new_first_norms: float32 [4, 2048], P(None, 'dp')
- new_second_norms: float32 [4, 2048], P(None, 'dp')
- new_norms: float32 [4, 2048], P(None, 'dp')
- copy_norms: bfloat16 [4, 2048], P(None, 'dp')
The draws below stay inside these ranges and needn't reach their ends.
Inputs may be any that keep to these rules, and one draw needn't show every extreme that they name: `prefix_lens`: the shared prefix of a group. `solution_lens`: only the first group_sizes[g] slots of row g count. The prefix and those solutions fill between 256 and 512 positions of their group, exactly 512 in some group; the remaining positions are padding. `norms`: gains lie between 0.5 and 1.5, shifts between -0.9 and 0.9. `first_qkv`: no entry is zero. `second_qkv`: all entries are positive. `first_out`: no entry is zero. `second_out`: all entries are positive. `first_up`: no entry is zero. `second_up`: all entries are positive. `first_down`: no entry is zero. `second_down`: all entries are positive. `first_norms`: no entry is zero. `second_norms`: all entries are positive.
All inputs are finite; a program needn't handle non-finite values.
Results may differ from the reference program's by a relative error of at most 0.014.
The reference program's roundings to bfloat16 on the way count: a program that leaves them out, or rounds other values in their place, can miss the bound.
Values may be sent and summed in bfloat16 or wider, within the bound.
A program may use at most 128 MiB of HBM per device.

```python
import math
import jax
import jax.numpy as jnp
from jax import lax

D = 2048
HEADS = 16
HD = 128
FF = 8192
GTOK = 512
SLOTS = 16
STEP = 5
GROUPS = 16
TOKENS = 8192


def group_plan(key):
    parts = jax.random.split(key, 6)
    groups_at = jnp.arange(GROUPS)
    fullest = jax.random.randint(parts[1], (), 0, GROUPS)
    widest = (fullest + 1) % GROUPS
    is_full = groups_at == fullest
    sizes = jax.random.randint(parts[0], (GROUPS,), 4, SLOTS + 1)
    sizes = jnp.where(is_full, 4, sizes)
    used = jax.random.randint(parts[2], (GROUPS,), GTOK // 2, GTOK + 1)
    used = jnp.where(is_full, GTOK, used)
    prefix = jax.random.randint(parts[3], (GROUPS,), GTOK // 8, GTOK // 4 + 1)
    prefix = jnp.where(is_full, GTOK // 8, prefix)
    prefix = jnp.where(groups_at == widest, GTOK // 4, prefix)
    slot_live = jnp.arange(SLOTS)[None, :] < sizes[:, None]
    shares = jnp.where(slot_live, jax.random.randint(parts[4], (GROUPS, SLOTS), 1, 4), 0)
    shares = jnp.where(is_full[:, None], jnp.where(jnp.arange(SLOTS)[None, :] == 3, 1, 0), shares)
    room = used - prefix - sizes
    extra = room[:, None] * shares // jnp.maximum(jnp.sum(shares, axis=1), 1)[:, None]
    lens = jnp.where(slot_live, 1 + extra, 0)
    deficit = used - prefix - jnp.sum(lens, axis=1)
    is_last = jnp.arange(SLOTS)[None, :] == sizes[:, None] - 1
    lens = lens + jnp.where(is_last, deficit[:, None], 0)
    unused = jax.random.randint(parts[5], (GROUPS, SLOTS), 1, GTOK // 8 + 1)
    lens = jnp.where(slot_live, lens, unused)
    return (sizes.astype(jnp.int32), prefix.astype(jnp.int32), lens.astype(jnp.int32))


def signed_moment(key, shape, grad_size):
    key_sign, key_size = jax.random.split(key)
    signs = jax.random.randint(key_sign, shape, 0, 2).astype(jnp.float32) * 2.0 - 1.0
    magnitude = jax.random.uniform(key_size, shape, jnp.float32, 0.5, 1.5)
    return grad_size * signs * magnitude


def square_moment(key, shape, grad_size):
    factor = jnp.exp(jax.random.uniform(key, shape, jnp.float32, 0.0, math.log(4.0)))
    return grad_size * grad_size * factor


def attn_share():
    return (10.0 / GTOK) ** 0.5


def norm_sizes():
    base = math.sqrt(TOKENS)
    upper = 50.0 * attn_share() * base
    lower = 2.2 * base
    return jnp.array([upper, upper, lower, lower], jnp.float32)[:, None]


def draw_group_sizes(key, part):
    plan = group_plan(key)
    return plan[0]


def draw_prefix_lens(key, part):
    plan = group_plan(key)
    return plan[1]


def draw_solution_lens(key, part):
    plan = group_plan(key)
    return plan[2]


def draw_norms(key, part):
    key = jax.random.fold_in(key, 11)
    key_gain, key_shift = jax.random.split(key)
    gains = jax.random.uniform(key_gain, (4, D), jnp.float32, 0.5, 1.5)
    shifts = 0.3 * jnp.clip(jax.random.normal(key_shift, (4, D), jnp.float32), -3.0, 3.0)
    is_gain = (jnp.arange(4) % 2 == 0)[:, None]
    return jnp.where(is_gain, gains, shifts)


def draw_first_qkv(key, part):
    key = jax.random.fold_in(key, 21)
    return signed_moment(key, (3, D, D), 30.0 * attn_share() * math.sqrt(TOKENS))


def draw_second_qkv(key, part):
    key = jax.random.fold_in(key, 22)
    return square_moment(key, (3, D, D), 30.0 * attn_share() * math.sqrt(TOKENS))


def draw_first_out(key, part):
    key = jax.random.fold_in(key, 23)
    return signed_moment(key, (D, D), 3.6 * attn_share() * math.sqrt(TOKENS))


def draw_second_out(key, part):
    key = jax.random.fold_in(key, 24)
    return square_moment(key, (D, D), 3.6 * attn_share() * math.sqrt(TOKENS))


def draw_first_up(key, part):
    key = jax.random.fold_in(key, 25)
    return signed_moment(key, (D, FF), 1.2 * math.sqrt(TOKENS))


def draw_second_up(key, part):
    key = jax.random.fold_in(key, 26)
    return square_moment(key, (D, FF), 1.2 * math.sqrt(TOKENS))


def draw_first_down(key, part):
    key = jax.random.fold_in(key, 27)
    return signed_moment(key, (FF, D), 0.6 * math.sqrt(TOKENS))


def draw_second_down(key, part):
    key = jax.random.fold_in(key, 28)
    return square_moment(key, (FF, D), 0.6 * math.sqrt(TOKENS))


def draw_first_norms(key, part):
    key = jax.random.fold_in(key, 29)
    return signed_moment(key, (4, D), 1.0) * norm_sizes()


def draw_second_norms(key, part):
    key = jax.random.fold_in(key, 30)
    return square_moment(key, (4, D), 1.0) * norm_sizes() * norm_sizes()


def level_of(stream_key, dims, cuts, least, high):
    def one(axis_at, shards_of):
        draws = jax.random.uniform(jax.random.fold_in(jax.random.fold_in(stream_key, 6), axis_at), (shards_of,), jnp.float32, least / len(cuts), high / len(cuts))
        return jnp.repeat(jnp.exp(draws), dims[axis_at] // shards_of).reshape((-1,) + (1,) * (len(dims) - axis_at - 1))

    loudness = one(*cuts[0])
    for cut in cuts[1:]:
        loudness = loudness * one(*cut)
    return loudness


def noise(rng, dims, width, limit, pieces=(), kind=jnp.bfloat16):
    result = width * jax.random.normal(rng, dims, jnp.float32)
    if pieces:
        result = result * level_of(rng, dims, pieces, -0.22, 0.18)
    return jnp.clip(result, -limit, limit).astype(kind)


def setup_inputs(seed: int = 0) -> dict:
    keys = jax.random.split(jax.random.key(seed), 21)
    return {
        "tokens": noise(keys[0], (TOKENS, D), 1.0, 6.0, ((0, 16),)),
        "cotangent": noise(keys[1], (TOKENS, D), 1.0, 6.0, ((0, 16),)),
        "group_sizes": draw_group_sizes(jax.random.fold_in(keys[20], 71), 0),
        "prefix_lens": draw_prefix_lens(jax.random.fold_in(keys[20], 71), 0),
        "solution_lens": draw_solution_lens(jax.random.fold_in(keys[20], 71), 0),
        "w_qkv": noise(keys[5], (3, D, D), D ** -0.5, 0.125, ((1, 16), (2, 8)), jnp.float32),
        "w_out": noise(keys[6], (D, D), (D // 64) ** -0.5, 1.0, ((0, 8), (1, 16)), jnp.float32),
        "w_up": noise(keys[7], (D, FF), D ** -0.5, 0.125, ((0, 16), (1, 8)), jnp.float32),
        "w_down": noise(keys[8], (FF, D), (FF // 16) ** -0.5, 0.25, ((0, 8), (1, 16)), jnp.float32),
        "norms": draw_norms(jax.random.fold_in(keys[20], 71), 0),
        "first_qkv": draw_first_qkv(jax.random.fold_in(keys[20], 71), 0),
        "second_qkv": draw_second_qkv(jax.random.fold_in(keys[20], 71), 0),
        "first_out": draw_first_out(jax.random.fold_in(keys[20], 71), 0),
        "second_out": draw_second_out(jax.random.fold_in(keys[20], 71), 0),
        "first_up": draw_first_up(jax.random.fold_in(keys[20], 71), 0),
        "second_up": draw_second_up(jax.random.fold_in(keys[20], 71), 0),
        "first_down": draw_first_down(jax.random.fold_in(keys[20], 71), 0),
        "second_down": draw_second_down(jax.random.fold_in(keys[20], 71), 0),
        "first_norms": draw_first_norms(jax.random.fold_in(keys[20], 71), 0),
        "second_norms": draw_second_norms(jax.random.fold_in(keys[20], 71), 0),
    }


PRECISE = lax.Precision.HIGHEST
NEG_FILL = -1e+30
BETA_ONE = 0.5
BETA_TWO = 0.5
ADAM_EPS = 1e-08
NORM_EPS = 1e-05
DECAY_RATE = 0.1
RATE_QKV = 0.02
RATE_OUT = 0.15
RATE_UP = 0.02
RATE_DOWN = 0.01
RATE_NORMS = 0.3

@jax.custom_vjp
def low(v):
    return lax.optimization_barrier(v.astype(jnp.bfloat16)).astype(jnp.float32)

@jax.custom_vjp
def low_back(v):
    return v

def low_keep(v):
    return (low(v), None)

def low_pass(kept, grad):
    return (grad,)

def back_keep(v):
    return (v, None)

def back_low(kept, grad):
    return (low(grad),)
low.defvjp(low_keep, low_pass)
low_back.defvjp(back_keep, back_low)

def layer_norm(inputs, norm_gain, norm_shift):
    row_mean = lax.optimization_barrier(jnp.mean(inputs, axis=-1, keepdims=True))
    centered = inputs - row_mean
    spread = lax.optimization_barrier(jnp.mean(centered * centered, axis=-1, keepdims=True))
    return centered * lax.rsqrt(spread + NORM_EPS) * norm_gain + norm_shift

def layout(group_size, prefix_len, slot_lens, length):
    slot_count = slot_lens.shape[0]
    slot_live = jnp.arange(slot_count, dtype=jnp.int32) < group_size
    counted = jnp.where(slot_live, slot_lens, 0).astype(jnp.int32)
    seg_ends = (prefix_len + jnp.cumsum(counted)).astype(jnp.int32)
    position = jnp.arange(length, dtype=jnp.int32)
    segment = lax.optimization_barrier(jnp.sum((position[:, None] >= seg_ends[None, :]).astype(jnp.int32), axis=1))
    segment = jnp.where(position < prefix_len, -1, segment)
    valid_rows = position < seg_ends[slot_count - 1]
    linked = (segment[:, None] == segment[None, :]) | (segment[None, :] < 0)
    causal = position[None, :] <= position[:, None]
    allowed = linked & causal & valid_rows[:, None] & valid_rows[None, :]
    allowed = allowed | (position[:, None] == position[None, :])
    return (allowed, valid_rows)

def attend(queries, key_rows, value_rows, allowed):
    length = queries.shape[0]
    head_q = queries.reshape(length, HEADS, HD)
    head_k = key_rows.reshape(length, HEADS, HD)
    head_v = value_rows.reshape(length, HEADS, HD)
    scores = low_back(jnp.einsum('qhd,khd->hqk', head_q, head_k, precision=PRECISE))
    scores = jnp.where(allowed[None, :, :], scores, NEG_FILL)
    row_top = lax.optimization_barrier(jnp.max(scores, axis=-1, keepdims=True))
    weights = jnp.exp(scores - row_top)
    probs_low = low(weights / lax.optimization_barrier(jnp.sum(weights, axis=-1, keepdims=True)))
    mixed = jnp.einsum('hqk,khd->qhd', probs_low, head_v, precision=PRECISE)
    return mixed.reshape(length, HEADS * HD)

def adamw(weight, grad_in, first_old, second_old, step_rate, weight_decay):
    first_new = BETA_ONE * first_old + (1.0 - BETA_ONE) * grad_in
    second_new = BETA_TWO * second_old + (1.0 - BETA_TWO) * grad_in * grad_in
    corr_one = 1.0 - BETA_ONE ** STEP
    corr_two = 1.0 - BETA_TWO ** STEP
    step_dir = first_new / corr_one / (jnp.sqrt(second_new / corr_two) + ADAM_EPS)
    weight_new = weight - step_rate * (step_dir + weight_decay * weight)
    return (grad_in, first_new, second_new, weight_new, weight_new.astype(jnp.bfloat16))

def rounded(master):
    return lax.optimization_barrier(master.astype(jnp.bfloat16)).astype(jnp.float32)

def reference(tokens, cotangent, group_sizes, prefix_lens, solution_lens, w_qkv, w_out, w_up, w_down, norms, first_qkv, second_qkv, first_out, second_out, first_up, second_up, first_down, second_down, first_norms, second_norms):
    allowed, valid_rows = jax.vmap(lambda size_one, prefix_one, lens_one: layout(size_one, prefix_one, lens_one, GTOK))(group_sizes, prefix_lens, solution_lens)
    row_mask = valid_rows.reshape(TOKENS).astype(jnp.float32)
    score_scale = HD ** (-0.5)

    def forward(inputs, qkv_used, out_used, up_used, down_used, norms_used):
        normed_one = low(layer_norm(inputs, norms_used[0], norms_used[1]))
        queries = low_back(low(jnp.dot(normed_one, qkv_used[0], precision=PRECISE) * score_scale))
        key_rows = low_back(low(jnp.dot(normed_one, qkv_used[1], precision=PRECISE)))
        value_rows = low_back(low(jnp.dot(normed_one, qkv_used[2], precision=PRECISE)))
        grouped = lambda field: field.reshape(GROUPS, GTOK, D)
        mixed = lax.map(jax.checkpoint(lambda group_item: attend(*group_item)), (grouped(queries), grouped(key_rows), grouped(value_rows), allowed))
        mixed_low = low_back(low(mixed.reshape(TOKENS, D)))
        attn_out = low_back(jnp.dot(mixed_low, out_used, precision=PRECISE))
        resid_one = inputs + attn_out
        normed_two = low(layer_norm(resid_one, norms_used[2], norms_used[3]))
        up_pre = low_back(jnp.dot(normed_two, up_used, precision=PRECISE))
        hidden = low(jax.nn.gelu(up_pre, approximate=True))
        return resid_one + jnp.dot(hidden, down_used, precision=PRECISE)
    block_full, pull_back = jax.vjp(forward, tokens.astype(jnp.float32), rounded(w_qkv), rounded(w_out), rounded(w_up), rounded(w_down), rounded(norms))
    back_rows = cotangent.astype(jnp.float32) * row_mask[:, None]
    input_grad, grad_qkv, grad_out, grad_up, grad_down, grad_norm_rows = pull_back(back_rows)
    qkv_res = adamw(w_qkv, grad_qkv, first_qkv, second_qkv, RATE_QKV, DECAY_RATE)
    out_res = adamw(w_out, grad_out, first_out, second_out, RATE_OUT, DECAY_RATE)
    up_res = adamw(w_up, grad_up, first_up, second_up, RATE_UP, DECAY_RATE)
    down_res = adamw(w_down, grad_down, first_down, second_down, RATE_DOWN, DECAY_RATE)
    norm_res = adamw(norms, grad_norm_rows, first_norms, second_norms, RATE_NORMS, 0.0)
    return (block_full.astype(jnp.bfloat16), input_grad, qkv_res[0], qkv_res[1], qkv_res[2], qkv_res[3], qkv_res[4], out_res[0], out_res[1], out_res[2], out_res[3], out_res[4], up_res[0], up_res[1], up_res[2], up_res[3], up_res[4], down_res[0], down_res[1], down_res[2], down_res[3], down_res[4], norm_res[0], norm_res[1], norm_res[2], norm_res[3], norm_res[4])
```

```python
import functools

import jax
import jax.numpy as jnp
from jax import lax
from jax.experimental import pallas as pl
from jax.experimental.pallas import tpu as pltpu
from jax.sharding import PartitionSpec as P

HD = 128
STEP = 5
ROWS = 512
D = 2048
NEG_FILL = -1e30
BETA_ONE = 0.5
BETA_TWO = 0.5
ADAM_EPS = 1e-08
NORM_EPS = 1e-05
DECAY_RATE = 0.1
RATE_QKV = 0.02
RATE_OUT = 0.15
RATE_UP = 0.02
RATE_DOWN = 0.01
RATE_NORMS = 0.3
SCALE = HD ** (-0.5)
GELU_K = 0.7978845608028654
GELU_C = 0.044715

BF = jnp.bfloat16
F32 = jnp.float32
MESH = pl.DeviceIdType.MESH
NT = (((1,), (1,)), ((), ()))
TN = (((0,), (0,)), ((), ()))
NN = (((1,), (0,)), ((), ()))

SHARD = ((128, 256), (128, 256), (128, 256), (256, 128), (128, 1024), (1024, 128))
GATHER_X_FIRST = (True, True, False, False, True, False)
REDUCE_Y_FIRST = (True, True, False, False, False, True)
Q_, K_, V_, O_, U_, D_ = range(6)


def dot(a, b, dims=NN):
    return lax.dot_general(a, b, dims, preferred_element_type=F32)


def ds(start, size, mult=None):
    if not isinstance(start, int):
        start = pl.multiple_of(start, mult or size)
    return pl.ds(start, size)


class Counter:
    def __init__(self):
        self.n = 0

    def take(self, k=1):
        base = self.n
        self.n += k
        return base


def kernel(*refs):
    it = iter(refs)
    take = lambda n: [next(it) for _ in range(n)]
    tok_h, back_h, bias_h, nrm_in = take(4)
    wq_h, wo_h, wu_h, wd_h = take(4)
    bo_h, ig_h, gqkv_o, go_o, gu_o, gd_o, gn_o, r1u_h, r1d_h = take(9)
    wf_q, wf_o, wf_u, wf_d = take(4)
    own = take(6)
    gat = take(6)
    rcv1 = take(4) + [r1u_h, r1d_h]
    mid = take(6)
    rcv2 = take(6)
    (tile, tok, back, bias, a1, qkv, mixed, probs, a2, hid, dup, dhid, ps_a, ps_b) = take(14)
    rc = take(4)
    rz = take(4)
    (dt, r1, dr1, ybuf, dqkv, pb_s, ds_s, nst, nbuf, gains, ngrad, nrec, oblk_b, oblk_i) = take(14)
    ssem, rsem, lsem = take(3)

    d_at = lax.axis_index("dp")
    t_at = lax.axis_index("tensor")
    x = d_at // 4
    yl = (d_at // 2) % 2
    c = d_at % 2
    z = t_at // 2
    yh = t_at % 2
    y = yh * 2 + yl
    other = 1 - c

    def dev(px, py, pz, pc):
        return {"dp": (px * 2 + py % 2) * 2 + pc, "tensor": pz * 2 + py // 2}

    ns, nr, nl = Counter(), Counter(), Counter()
    pending = []

    def rcopy(src, dst, to, si, ri):
        return pltpu.make_async_remote_copy(
            src_ref=src, dst_ref=dst, send_sem=ssem.at[si], recv_sem=rsem.at[ri],
            device_id=to, device_id_type=MESH)

    def send(src, dst, to, ri, tag=""):
        cp = rcopy(src, dst, to, ns.take(), ri)
        cp.start()
        pending.append((tag, cp, None))

    def send_or_local(here, src, dst, to, ri, tag=""):
        cp = rcopy(src, dst, to, ns.take(), ri)
        away = jnp.logical_not(here)

        @pl.when(here)
        def _():
            pltpu.make_async_copy(src, dst, rsem.at[ri]).start()

        @pl.when(away)
        def _():
            cp.start()

        pending.append((tag, cp, away))

    def send_if(cond, src, dst, to, ri, tag=""):
        cp = rcopy(src, dst, to, ns.take(), ri)

        @pl.when(cond)
        def _():
            cp.start()

        pending.append((tag, cp, cond))

    def flush(tag=None):
        for item in pending[:]:
            kind, cp, cond = item
            if tag is None or kind == tag:
                pending.remove(item)
                if cond is None:
                    cp.wait_send()
                else:
                    pl.when(cond)(cp.wait_send)

    def got(dst, ri):
        rcopy(dst, dst, dev(x, y, z, other), 0, ri).wait_recv()

    loads = []

    def load(src, dst):
        cp = pltpu.make_async_copy(src, dst, lsem.at[nl.take()])
        cp.start()
        loads.append(cp)
        return cp

    ld_q = load(wq_h, wf_q)
    ld_o = load(wo_h, wf_o)
    ld_u = load(wu_h, wf_u)
    ld_d = load(wd_h, wf_d)

    yp = yh * 2 + (1 - yl)
    peers = [dev(x, y, z, other)]
    for k in (1, 2, 3):
        for cc in (0, 1):
            peers.append(dev((x + k) % 4, y, z, cc))
            peers.append(dev(x, (y + k) % 4, z, cc))
            peers.append(dev(x, y, (z + k) % 4, cc))
            peers.append(dev((x + k) % 4, yp, z, cc))
    barrier = pltpu.get_barrier_semaphore()
    for peer in peers:
        pl.semaphore_signal(barrier, inc=1, device_id=peer, device_id_type=MESH)
    nst[0:4, :] = nrm_in[...].astype(BF).astype(F32)
    nst[4:8, :] = jnp.zeros((4, 128), F32)
    ld_q.wait()
    for j in range(3):
        own[j][...] = wf_q[j].astype(BF)
    ld_o.wait()
    own[O_][...] = wf_o[...].astype(BF)
    pl.semaphore_wait(barrier, len(peers))

    tok_r = nr.take(3)
    group_in = ((tok_h, tok), (bias_h, bias), (back_h, back))
    home = c == yh

    def share(i):
        src, dst = group_in[i]
        send_if(home, src, dst, dev(x, y, z, other), tok_r + i)

        @pl.when(home)
        def _():
            pltpu.make_async_copy(src, dst, rsem.at[tok_r + i]).start()

    norm_r = nr.take(16)
    for dx in range(4):
        for dl in (0, 1):
            for dc in (0, 1):
                if dx or dl or dc:
                    to = dev((x + dx) % 4, yh * 2 + (yl + dl) % 2, z, (c + dc) % 2)
                    send(nst, nbuf.at[d_at], to, norm_r + d_at)

    g1_r = [nr.take(8) for _ in range(6)]
    g2_r = [nr.take(4) for _ in range(6)]

    def gather_one(k):
        for j in range(4):
            if GATHER_X_FIRST[k]:
                px = (x + j) % 4
                slot, to = g1_r[k] + x * 2 + c, dev(px, y, z, yh)
            else:
                py = (y + j) % 4
                slot, to = g1_r[k] + yl * 2 + c, dev(x, py, z, yh)
            dst = gat[k].at[x, yl, c]
            if j == 0:
                send_or_local(home, own[k], dst, to, slot, "gather")
            else:
                send(own[k], dst, to, slot, "gather")

    r_at = (y + 4 - 2 * c) % 4

    def gather_two(k):
        if GATHER_X_FIRST[k]:
            @pl.when(home)
            def _():
                for sx in range(4):
                    for sc in range(2):
                        got(gat[k].at[sx, yl, sc], g1_r[k] + sx * 2 + sc)

            part = gat[k].at[:, yl]
            for step in (1, 3):
                send_if(home, part, part, dev(x, (y + step) % 4, z, c), g2_r[k], "gather")
        else:
            for sl in range(2):
                for sc in range(2):
                    got(gat[k].at[x, sl, sc], g1_r[k] + sl * 2 + sc)
            part = gat[k].at[x]
            send(part, part, dev((x + 1) % 4, y, z, c), g2_r[k], "gather")
            send(part, part, dev((x + 3) % 4, y, z, c), g2_r[k] + 1, "gather")

    def gather_three(k):
        if GATHER_X_FIRST[k]:
            src_l = 1 - r_at % 2
            got(gat[k].at[:, src_l], g2_r[k])
            half = jnp.where((r_at == 0) | (r_at == 3), 1, 0)
            part = gat[k].at[pl.ds(2 * half, 2), src_l]
            to = dev(x, (2 * c + 3 - r_at % 2) % 4, z, c)
            send(part, part, to, g2_r[k] + 1 + half, "gather")
        else:
            xm, xp = (x + 3) % 4, (x + 1) % 4
            got(gat[k].at[xm], g2_r[k])
            part = gat[k].at[xm, 0]
            send(part, part, dev(xp, y, z, c), g2_r[k] + 2, "gather")
            got(gat[k].at[xp], g2_r[k] + 1)
            part = gat[k].at[xp, 1]
            send(part, part, dev(xm, y, z, c), g2_r[k] + 3, "gather")

    def gather_end(k):
        if GATHER_X_FIRST[k]:
            @pl.when(r_at >= 2)
            def _():
                for half in range(2):
                    got(gat[k].at[pl.ds(2 * half, 2), r_at % 2], g2_r[k] + 1 + half)
        else:
            x2 = (x + 2) % 4
            got(gat[k].at[x2, 0], g2_r[k] + 2)
            got(gat[k].at[x2, 1], g2_r[k] + 3)

    share(0)
    for k in (Q_, K_, V_, O_):
        gather_one(k)
    ld_u.wait()

    @pl.loop(0, 8)
    def _(i):
        own[U_][ds(i * 16, 16), :] = wf_u[ds(i * 16, 16), :].astype(BF)

    ld_d.wait()

    @pl.loop(0, 8)
    def _(i):
        own[D_][ds(i * 128, 128), :] = wf_d[ds(i * 128, 128), :].astype(BF)

    for dx in range(4):
        for dl in (0, 1):
            for dc in (0, 1):
                if dx or dl or dc:
                    sd = (((x + dx) % 4) * 2 + (yl + dl) % 2) * 2 + (c + dc) % 2
                    got(nbuf.at[sd], norm_r + sd)
    nbuf[d_at] = nst[...]
    for i in range(16):
        gains[:, i * 128:(i + 1) * 128] = nbuf[i]

    got(tok, tok_r)

    @pl.loop(0, ROWS // 32)
    def _(i):
        rows = ds(i * 32, 32)
        v = tok[rows, :].astype(F32)
        cen = v - jnp.mean(v, axis=-1, keepdims=True)
        var = jnp.mean(cen * cen, axis=-1, keepdims=True)
        a1[rows, :] = (cen * lax.rsqrt(var + NORM_EPS) * gains[0:1, :] + gains[1:2, :]).astype(BF)

    for k in (Q_, K_, V_, O_):
        gather_two(k)
    share(1)
    share(2)
    gather_one(U_)
    gather_one(D_)
    for k in (Q_, K_, V_, O_):
        gather_three(k)

    def project(j):
        gather_end(j)

        @pl.loop(0, 2)
        def _(i):
            rows = ds(i * 256, 256)
            v = dot(a1[rows, :], gat[j][...].reshape(D, 256))
            if j == Q_:
                v = v * SCALE
            qkv[j, rows, :] = v.astype(BF)

    project(Q_)
    project(K_)
    project(V_)
    gather_two(U_)
    gather_two(D_)
    got(bias, tok_r + 1)

    for h in range(2):
        cols = slice(h * HD, (h + 1) * HD)

        @pl.loop(0, 4)
        def _(i):
            rows = ds(i * 128, 128)
            s = dot(qkv[0, rows, cols], qkv[1, :, cols], NT) + bias[rows, :].astype(F32)
            w = jnp.exp(s - jnp.max(s, axis=-1, keepdims=True))
            p = w / jnp.sum(w, axis=-1, keepdims=True)
            probs[h, rows, :] = p
            mixed[rows, cols] = dot(p.astype(BF), qkv[2, :, cols]).astype(BF)

    my_row = c * 256 + z * 64
    rc_r = [nr.take() for _ in range(4)]
    rz_r = [nr.take(3) for _ in range(4)]

    def sum_start(k, ps, compute):
        lo = other * 256
        compute(lo)
        half = ps.at[ds(lo, 256), :]
        send(half, rc[k], dev(x, y, z, other), rc_r[k], f"sum{k}")
        compute(c * 256)

    def sum_middle(k, ps):
        got(rc[k], rc_r[k])
        for dz in (2, 1, 3, 0):
            pz = (z + dz) % 4
            base = c * 256 + pz * 64

            @pl.loop(0, 4)
            def _(i):
                rows = ds(base + i * 16, 16)
                from_other = rc[k][ds(pz * 64 + i * 16, 16), :].astype(F32)
                ps[rows, :] = (ps[rows, :].astype(F32) + from_other).astype(BF)

            if dz:
                send(ps.at[ds(base, 64), :], rz[k].at[dz - 1], dev(x, y, pz, c), rz_r[k] + dz - 1, f"sum{k}")

    def sum_wait(k):
        for dz in (1, 3, 2):
            got(rz[k].at[dz - 1], rz_r[k] + dz - 1)

    def sum_rows(k, ps, i):
        rows = ds(i * 16, 16)
        v = ps[ds(my_row + i * 16, 16), :].astype(F32)
        for j in range(3):
            v = v + rz[k][j, rows, :].astype(F32)
        return v

    ag_r = [nr.take(3) for _ in range(2)]
    ac_r = [nr.take(4) for _ in range(2)]

    def spread_start(k, buf):
        part = buf.at[ds(my_row, 64), :]
        for dz in (2, 1, 3):
            send(part, part, dev(x, y, (z + dz) % 4, c), ag_r[k] + dz - 1)
        send(part, part, dev(x, y, z, other), ac_r[k] + z)

    def spread_pass(k, buf):
        for dz in (1, 3, 2):
            sz = (z + 4 - dz) % 4
            part = buf.at[ds(c * 256 + sz * 64, 64), :]
            got(part, ag_r[k] + dz - 1)
            send(part, part, dev(x, y, z, other), ac_r[k] + sz)

    def spread_end(k, buf):
        for sz in range(4):
            got(buf.at[ds(other * 256 + sz * 64, 64), :], ac_r[k] + sz)

    def attn_out(lo):
        gather_end_once(O_)

        @pl.loop(0, 4)
        def _(i):
            cols = [gat[O_][i, a, b] for a in range(2) for b in range(2)]
            v = dot(mixed[ds(lo, 256), :], jnp.concatenate(cols, axis=1))
            ps_a[ds(lo, 256), ds(i * 512, 512)] = v.astype(BF)

    done = set()

    def gather_end_once(k):
        if k not in done:
            done.add(k)
            gather_end(k)

    sum_start(0, ps_a, attn_out)
    sum_middle(0, ps_a)
    gather_three(U_)
    gather_three(D_)
    sum_wait(0)

    @pl.loop(0, 4)
    def _(i):
        rows = ds(i * 16, 16)
        v = tok[ds(my_row + i * 16, 16), :].astype(F32) + sum_rows(0, ps_a, i)
        r1[rows, :] = v
        cen = v - jnp.mean(v, axis=-1, keepdims=True)
        var = jnp.mean(cen * cen, axis=-1, keepdims=True)
        n = cen * lax.rsqrt(var + NORM_EPS) * gains[2:3, :] + gains[3:4, :]
        a2[ds(my_row + i * 16, 16), :] = n.astype(BF)

    spread_start(0, a2)
    spread_pass(0, a2)

    got(back, tok_r + 2)
    gather_end(D_)

    @pl.loop(0, 4)
    def _(i):
        hrows = ds(i * 256, 256)
        w = jnp.concatenate([gat[D_][a, b, e, hrows, :] for a in range(4) for b in range(2) for e in range(2)], axis=1)
        dhid[:, hrows] = dot(back[...], w, NT)

    gather_end(U_)
    spread_end(0, a2)

    @pl.loop(0, 4)
    def _(i):
        cols = ds(i * 256, 256)
        u = dot(a2[...], gat[U_][:, :, :, :, cols].reshape(D, 256))
        th = jnp.tanh(GELU_K * (u + GELU_C * u * u * u))
        hid[:, cols] = (0.5 * u * (1.0 + th)).astype(BF)
        slope = 0.5 * (1.0 + th) + 0.5 * u * (1.0 - th * th) * (GELU_K * (1.0 + 3.0 * GELU_C * u * u))
        dup[:, cols] = (dhid[:, cols] * slope).astype(BF)

    def entry(lo):
        @pl.loop(0, 4)
        def _(i):
            w = gat[U_][i].reshape(512, 1024)
            ps_a[ds(lo, 256), ds(i * 512, 512)] = dot(dup[ds(lo, 256), :], w, NT).astype(BF)

    def down(lo):
        @pl.loop(0, 4)
        def _(i):
            w = jnp.concatenate([gat[D_][i, a, b] for a in range(2) for b in range(2)], axis=1)
            ps_b[ds(lo, 256), ds(i * 512, 512)] = dot(hid[ds(lo, 256), :], w).astype(BF)

    flush("sum0")
    sum_start(1, ps_a, entry)
    sum_middle(1, ps_a)
    sum_start(2, ps_b, down)

    s1_r = [nr.take(4) for _ in range(6)]
    s2_r = [nr.take(4) for _ in range(6)]

    def scatter_one(k):
        if REDUCE_Y_FIRST[k]:
            for tl in range(2):
                for tc in range(2):
                    here = home & (yl == tl) & (c == tc)
                    src, dst = gat[k].at[:, tl, tc], rcv1[k].at[y]
                    send_or_local(here, src, dst, dev(x, 2 * c + tl, z, tc), s1_r[k] + y)
        else:
            for dx in (2, 1, 3):
                px = (x + dx) % 4
                send(gat[k].at[px], rcv1[k].at[dx - 1], dev(px, y, z, c), s1_r[k] + dx - 1)

    def add_up(parts, out, shape, scale=None):
        step = 16384 // shape[1]

        @pl.loop(0, shape[0] // step)
        def _(i):
            rows = ds(i * step, step)
            v = parts[0][rows, :].astype(F32)
            for p in parts[1:]:
                v = v + p[rows, :].astype(F32)
            if scale is not None:
                v = v * scale
            out[rows, :] = v.astype(out.dtype)

    def scatter_two(k):
        in_hbm = k in (U_, D_)
        if REDUCE_Y_FIRST[k]:
            for sy in range(4):
                got(rcv1[k].at[sy], s1_r[k] + sy)
            places = [(x + dx) % 4 for dx in (2, 1, 3, 0)]
            pick = [lambda p, sy=sy: rcv1[k].at[sy, p] for sy in range(4)]
        else:
            for j in range(3):
                got(rcv1[k].at[j], s1_r[k] + j)
            places = [(a, b) for a in range(2) for b in range(2)]
            pick = [lambda p, j=j: rcv1[k].at[j, p[0], p[1]] for j in range(3)]
        copies = []
        if in_hbm:
            base = nl.take(8)

            def fetch(i):
                cps = []
                for j, f in enumerate(pick):
                    cp = pltpu.make_async_copy(
                        f(places[i]), tiles(k, i % 2, j), lsem.at[base + (i % 2) * 4 + j])
                    cp.start()
                    cps.append(cp)
                return cps

            copies = fetch(0)
        for i, place in enumerate(places):
            if in_hbm:
                for cp in copies:
                    cp.wait()
                parts = [tiles(k, i % 2, j) for j in range(len(pick))]
                if i + 1 < len(places):
                    copies = fetch(i + 1)
            else:
                parts = [f(place) for f in pick]
            if REDUCE_Y_FIRST[k]:
                out = mid[k].at[place]
                add_up(parts, out, SHARD[k])
                to = dev(place, y, z, c)
                if i == 3:
                    pltpu.make_async_copy(out, rcv2[k].at[x], rsem.at[s2_r[k] + x]).start()
                else:
                    send(out, rcv2[k].at[x], to, s2_r[k] + x)
            else:
                out = mid[k].at[place[0], place[1]]
                add_up(parts + [gat[k].at[x, place[0], place[1]]], out, SHARD[k])
                here = home & (yl == place[0]) & (c == place[1])
                send_or_local(here, out, rcv2[k].at[y], dev(x, 2 * c + place[0], z, place[1]), s2_r[k] + y)

    def tiles(k, slot, j):
        return (tile_u if k == U_ else tile_d).at[slot, j]

    tile_u, tile_d = tile

    def scatter_end(k, out, scale=None):
        for j in range(4):
            got(rcv2[k].at[j], s2_r[k] + j)
        add_up([rcv2[k].at[j] for j in range(4)], out, SHARD[k], scale)

    flush("gather")

    @pl.loop(0, 8)
    def _(i):
        v = dot(hid[...], back[:, ds(i * 256, 256)], TN).astype(BF)
        a, b = i // 2, i % 2
        gat[D_][a, b, 0] = v[:, :128]
        gat[D_][a, b, 1] = v[:, 128:]

    scatter_one(D_)
    sum_middle(2, ps_b)

    @pl.loop(0, 8)
    def _(i):
        a, b = i // 2, i % 2
        v = dot(a2[:, ds(i * 256, 256)], dup[...], TN).astype(BF)
        gat[U_][a, b, 0] = v[:128]
        gat[U_][a, b, 1] = v[128:]

    scatter_one(U_)

    def norm_back(v, dy, gain):
        cen = v - jnp.mean(v, axis=-1, keepdims=True)
        rs = lax.rsqrt(jnp.mean(cen * cen, axis=-1, keepdims=True) + NORM_EPS)
        xh = cen * rs
        e = dy * gain
        dv = rs * (e - jnp.mean(e, axis=-1, keepdims=True) - xh * jnp.mean(e * xh, axis=-1, keepdims=True))
        return dv, jnp.sum(dy * xh, axis=0, keepdims=True), jnp.sum(dy, axis=0, keepdims=True)

    ngrad[...] = jnp.zeros_like(ngrad)
    sum_wait(1)

    @pl.loop(0, 4)
    def _(i):
        rows = ds(i * 16, 16)
        mine = ds(my_row + i * 16, 16)
        dv, dg, db = norm_back(r1[rows, :], sum_rows(1, ps_a, i), gains[2:3, :])
        v = back[mine, :].astype(F32) + dv
        dr1[rows, :] = v
        dt[mine, :] = v.astype(BF)
        ngrad[2:3, :] += dg
        ngrad[3:4, :] += db

    spread_start(1, dt)

    o1_r = [nr.take(8) for _ in range(2)]

    def out_start(k, blk, out):
        part = out.at[ds(my_row, 64), :]
        for dz in (2, 1, 3):
            send(blk, part, dev(x, y, (z + dz) % 4, yh), o1_r[k] + z * 2 + c)
        send_or_local(home, blk, part, dev(x, y, z, yh), o1_r[k] + z * 2 + c)
        y2 = (y + 2) % 4
        send(blk, part, dev(x, y2, z, yh), o1_r[k] + z * 2 + c)

    def out_pass(k, out):
        away = jnp.logical_not(home)
        for sc in range(2):
            part = out.at[ds(sc * 256 + z * 64, 64), :]

            @pl.when(away)
            def _():
                got(part, o1_r[k] + z * 2 + sc)

            for dz in (2, 1, 3):
                send_if(away, part, part, dev(x, y, (z + dz) % 4, c), o1_r[k] + z * 2 + sc)

    def out_end(k, out):
        away = jnp.logical_not(home)
        for sc in range(2):
            for dz in range(4):
                sz = (z + dz) % 4

                def wait_it():
                    got(out.at[ds(sc * 256 + sz * 64, 64), :], o1_r[k] + sz * 2 + sc)

                if dz == 0:
                    pl.when(home)(wait_it)
                else:
                    wait_it()

    spread_pass(1, dt)
    sum_wait(2)

    @pl.loop(0, 4)
    def _(i):
        rows = ds(i * 16, 16)
        oblk_b[rows, :] = (r1[rows, :] + sum_rows(2, ps_b, i)).astype(BF)

    spread_end(1, dt)

    @pl.loop(0, 2)
    def _(i):
        rows = ds(i * 256, 256)
        w = jnp.concatenate([gat[O_][a, b, e] for a in range(4) for b in range(2) for e in range(2)], axis=1)
        ybuf[rows, :] = dot(dt[rows, :], w, NT).astype(BF)

    for h in range(2):
        cols = slice(h * HD, (h + 1) * HD)

        @pl.loop(0, 4)
        def _(i):
            rows = ds(i * 128, 128)
            p = probs[h, rows, :]
            pb_s[rows, :] = p.astype(BF)
            dp = dot(ybuf[rows, cols], qkv[2, :, cols], NT)
            d_s = (p * (dp - jnp.sum(p * dp, axis=-1, keepdims=True))).astype(BF)
            ds_s[rows, :] = d_s
            dqkv[rows, cols] = dot(d_s, qkv[1, :, cols]).astype(BF)

        dqkv[:, 256 + h * HD:256 + (h + 1) * HD] = dot(ds_s[...], qkv[0, :, cols], TN).astype(BF)
        dqkv[:, 512 + h * HD:512 + (h + 1) * HD] = dot(pb_s[...], ybuf[:, cols], TN).astype(BF)

    def into_norm(lo):
        @pl.loop(0, 4)
        def _(i):
            ws = [gat[j][i].reshape(512, 256) for j in range(3)]
            v = dot(dqkv[ds(lo, 256), 0:256], ws[0], NT) * SCALE
            v = v + dot(dqkv[ds(lo, 256), 256:512], ws[1], NT)
            v = v + dot(dqkv[ds(lo, 256), 512:768], ws[2], NT)
            ps_a[ds(lo, 256), ds(i * 512, 512)] = v.astype(BF)

    flush("sum1")
    sum_start(3, ps_a, into_norm)
    sum_middle(3, ps_a)

    @pl.loop(0, 16)
    def _(i):
        a, b, e = i // 4, (i // 2) % 2, i % 2
        v = dot(a1[:, ds(i * 128, 128)], dqkv[...], TN)
        for j in range(3):
            w = v[:, j * 256:(j + 1) * 256]
            gat[j][a, b, e] = (w * SCALE if j == 0 else w).astype(BF)

    for k in (Q_, K_, V_):
        scatter_one(k)

    @pl.loop(0, 8)
    def _(i):
        v = dot(mixed[...], dt[:, ds(i * 256, 256)], TN).astype(BF)
        gat[O_][i // 2, i % 2, 0] = v[:, :128]
        gat[O_][i // 2, i % 2, 1] = v[:, 128:]

    scatter_one(O_)
    scatter_two(D_)
    scatter_two(U_)
    out_start(0, oblk_b, bo_h)

    sum_wait(3)

    @pl.loop(0, 4)
    def _(i):
        rows = ds(i * 16, 16)
        v = tok[ds(my_row + i * 16, 16), :].astype(F32)
        dv, dg, db = norm_back(v, sum_rows(3, ps_a, i), gains[0:1, :])
        oblk_i[rows, :] = (dr1[rows, :] + dv).astype(BF)
        ngrad[0:1, :] += dg
        ngrad[1:2, :] += db

    out_start(1, oblk_i, ig_h)

    n_r = [nr.take(7), nr.take(3), nr.take(3)]

    def norm_sum(stage, targets, base):
        for j, to in enumerate(targets):
            send(ngrad, nrec.at[base + j], to, n_r[stage] + j, "norm")
        flush("norm")
        for j in range(len(targets)):
            got(nrec.at[base + j], n_r[stage] + j)
        v = ngrad[...]
        for j in range(len(targets)):
            v = v + nrec[base + j]
        ngrad[...] = v

    norm_sum(0, [dev(x, y, (z + dz) % 4, (c + dc) % 2) for dz in range(4) for dc in range(2) if dz or dc], 0)
    for k in (Q_, K_, V_, O_):
        scatter_two(k)
    out_pass(0, bo_h)
    out_pass(1, ig_h)
    norm_sum(1, [dev((x + k) % 4, y, z, c) for k in (1, 2, 3)], 7)
    norm_sum(2, [dev(x, (y + k) % 4, z, c) for k in (1, 2, 3)], 10)
    gn_o[...] = ngrad[...]

    scatter_end(D_, gd_o)
    scatter_end(U_, gu_o)
    for j in range(3):
        scatter_end(j, gqkv_o.at[j])
    scatter_end(O_, go_o)
    out_end(0, bo_h)
    out_end(1, ig_h)
    flush()


def run_layer(tokens, back_rows, bias, norms, w_qkv, w_out, w_up, w_down):
    hbm = pl.BlockSpec(memory_space=pltpu.HBM)
    vmem = pl.BlockSpec(memory_space=pltpu.VMEM)
    shards = [(4, 2, 2) + s for s in SHARD]
    rcv1 = [(4, 4) + s if REDUCE_Y_FIRST[k] else (3, 2, 2) + s for k, s in enumerate(SHARD)]
    mid = [(4,) + s if REDUCE_Y_FIRST[k] else (2, 2) + s for k, s in enumerate(SHARD)]
    big = lambda s, t=BF: pltpu.VMEM(s, t)
    scratch = [big((3, 128, 256), F32), big((256, 128), F32), big((128, 1024), F32), big((1024, 128), F32)]
    scratch += [big(s) for s in SHARD]
    scratch += [big(s) for s in shards]
    scratch += [big(rcv1[k]) for k in (Q_, K_, V_, O_)]
    scratch += [big(s) for s in mid]
    scratch += [big((4,) + s) for s in SHARD]
    scratch += [
        [big((2, 3, 128, 1024)), big((2, 4, 1024, 128))],
        big((ROWS, D)), big((ROWS, D)), big((ROWS, ROWS)), big((ROWS, D)), big((3, ROWS, 256)),
        big((ROWS, 256)), big((2, ROWS, ROWS), F32), big((ROWS, D)), big((ROWS, 1024)), big((ROWS, 1024)),
        big((ROWS, 1024), F32), big((ROWS, D)), big((ROWS, D)),
    ]
    scratch += [big((256, D))] * 4
    scratch += [big((3, 64, D))] * 4
    scratch += [
        big((ROWS, D)), big((64, D), F32), big((64, D), F32), big((ROWS, 256)), big((ROWS, 768)),
        big((ROWS, ROWS)), big((ROWS, ROWS)), big((8, 128), F32), big((16, 8, 128), F32), big((8, D), F32),
        big((8, D), F32), big((13, 8, D), F32), big((64, D)), big((64, D)),
    ]
    scratch += [pltpu.SemaphoreType.DMA((260,)), pltpu.SemaphoreType.DMA((260,)), pltpu.SemaphoreType.DMA((32,))]
    out_shape = [
        jax.ShapeDtypeStruct((ROWS, D), BF), jax.ShapeDtypeStruct((ROWS, D), BF),
        jax.ShapeDtypeStruct((3, 128, 256), F32), jax.ShapeDtypeStruct((256, 128), F32),
        jax.ShapeDtypeStruct((128, 1024), F32), jax.ShapeDtypeStruct((1024, 128), F32),
        jax.ShapeDtypeStruct((8, D), F32),
        jax.ShapeDtypeStruct(rcv1[U_], BF), jax.ShapeDtypeStruct(rcv1[D_], BF),
    ]
    return pl.pallas_call(
        kernel,
        out_shape=out_shape,
        in_specs=[hbm, hbm, hbm, vmem, hbm, hbm, hbm, hbm],
        out_specs=[hbm, hbm, vmem, vmem, vmem, vmem, vmem, hbm, hbm],
        scratch_shapes=scratch,
        compiler_params=pltpu.CompilerParams(
            collective_id=0, has_side_effects=True, vmem_limit_bytes=63 * 2**20),
    )(tokens, back_rows, bias, norms, w_qkv, w_out, w_up, w_down)[:7]


def layout(group_size, prefix_len, slot_lens, length):
    slot_count = slot_lens.shape[0]
    slot_live = jnp.arange(slot_count, dtype=jnp.int32) < group_size
    counted = jnp.where(slot_live, slot_lens, 0)
    seg_ends = prefix_len + jnp.cumsum(counted)
    position = jnp.arange(length, dtype=jnp.int32)
    segment = jnp.sum((position[:, None] >= seg_ends[None, :]).astype(jnp.int32), axis=1)
    segment = jnp.where(position < prefix_len, -1, segment)
    valid_rows = position < seg_ends[slot_count - 1]
    linked = (segment[:, None] == segment[None, :]) | (segment[None, :] < 0)
    causal = position[None, :] <= position[:, None]
    allowed = linked & causal & valid_rows[:, None] & valid_rows[None, :]
    allowed = allowed | (position[:, None] == position[None, :])
    return (allowed, valid_rows)


def adamw(weight, grad_in, first_old, second_old, step_rate, weight_decay):
    first_new = BETA_ONE * first_old + (1.0 - BETA_ONE) * grad_in
    second_new = BETA_TWO * second_old + (1.0 - BETA_TWO) * grad_in * grad_in
    corr_one = 1.0 - BETA_ONE**STEP
    corr_two = 1.0 - BETA_TWO**STEP
    step_dir = first_new / corr_one / (jnp.sqrt(second_new / corr_two) + ADAM_EPS)
    weight_new = weight - step_rate * (step_dir + weight_decay * weight)
    return (grad_in, first_new, second_new, weight_new, weight_new.astype(jnp.bfloat16))


def per_device(
    tokens, cotangent, group_sizes, prefix_lens, solution_lens,
    w_qkv, w_out, w_up, w_down, norms,
    first_qkv, second_qkv, first_out, second_out,
    first_up, second_up, first_down, second_down, first_norms, second_norms,
):
    length = tokens.shape[0]
    allowed, valid_rows = layout(group_sizes[0], prefix_lens[0], solution_lens[0], length)
    bias = jnp.where(allowed, 0.0, NEG_FILL).astype(BF)
    back_rows = jnp.where(valid_rows[:, None], cotangent, jnp.zeros_like(cotangent))
    block_out, input_grad, grad_qkv, grad_out, grad_up, grad_down, grad_norms = run_layer(
        tokens, back_rows, bias, norms, w_qkv, w_out, w_up, w_down)
    at = lax.axis_index("dp") * 128
    grad_norm_rows = lax.dynamic_slice(grad_norms, (0, at), (4, 128))
    qkv_res = adamw(w_qkv, grad_qkv, first_qkv, second_qkv, RATE_QKV, DECAY_RATE)
    out_res = adamw(w_out, grad_out, first_out, second_out, RATE_OUT, DECAY_RATE)
    up_res = adamw(w_up, grad_up, first_up, second_up, RATE_UP, DECAY_RATE)
    down_res = adamw(w_down, grad_down, first_down, second_down, RATE_DOWN, DECAY_RATE)
    norm_res = adamw(norms, grad_norm_rows, first_norms, second_norms, RATE_NORMS, 0.0)
    return (block_out, input_grad.astype(F32), *qkv_res, *out_res, *up_res, *down_res, *norm_res)


def solution(mesh):
    row, mat = P("dp", None), P("tensor", "dp")
    qkv, up, nrm = P(None, "dp", "tensor"), P("dp", "tensor"), P(None, "dp")
    return jax.shard_map(
        per_device,
        mesh=mesh,
        in_specs=(row, row, P("dp"), P("dp"), row, qkv, mat, up, mat, nrm,
                  qkv, qkv, mat, mat, up, up, mat, mat, nrm, nrm),
        out_specs=(row, row) + (qkv,) * 5 + (mat,) * 5 + (up,) * 5 + (mat,) * 5 + (nrm,) * 5,
        check_vma=False,
    )
```

```python
import functools

import jax
import jax.numpy as jnp
from jax import lax
from jax.experimental import pallas as pl
from jax.experimental.pallas import tpu as pltpu
from jax.sharding import PartitionSpec as P

HD = 128
STEP = 5
ROWS = 512
D = 2048
NEG_FILL = -1e30
BETA_ONE = 0.5
BETA_TWO = 0.5
ADAM_EPS = 1e-08
NORM_EPS = 1e-05
DECAY_RATE = 0.1
RATE_QKV = 0.02
RATE_OUT = 0.15
RATE_UP = 0.02
RATE_DOWN = 0.01
RATE_NORMS = 0.3
SCALE = HD ** (-0.5)
GELU_K = 0.7978845608028654
GELU_C = 0.044715

BF = jnp.bfloat16
F32 = jnp.float32
MESH = pl.DeviceIdType.MESH
NT = (((1,), (1,)), ((), ()))
TN = (((0,), (0,)), ((), ()))
NN = (((1,), (0,)), ((), ()))

SHARD = ((128, 256), (128, 256), (128, 256), (256, 128), (128, 1024), (1024, 128))
Q_, K_, V_, O_, U_, D_ = range(6)
G_QKV = ((Q_, 0, 128, True), (K_, 0, 128, False), (V_, 0, 64, True), (V_, 64, 64, False))
G_OUT = ((O_, 0, 128, True), (O_, 128, 128, False))
G_UP = ((U_, 0, 64, True), (U_, 64, 64, False))
G_DOWN = ((D_, 0, 512, True), (D_, 512, 512, False))
GATHER = G_QKV + G_OUT + G_UP + G_DOWN
S_DOWN = ((D_, 0, 512, True), (D_, 512, 512, False))
S_UP = ((U_, 0, 64, True), (U_, 64, 64, False))
S_QKV = ((Q_, 0, 128, True), (K_, 0, 128, False), (V_, 0, 64, True), (V_, 64, 64, False))
S_OUT = ((O_, 0, 128, True), (O_, 128, 128, False))
SCATTER = S_DOWN + S_UP + S_QKV + S_OUT


def dot(a, b, dims=NN):
    return lax.dot_general(a, b, dims, preferred_element_type=F32)


def ds(start, size, mult=None):
    if not isinstance(start, int):
        start = pl.multiple_of(start, mult or size)
    return pl.ds(start, size)


N_SEND = 200
N_RECV = 140
N_LOCAL = 16


class Counter:
    def __init__(self):
        self.n = 0

    def take(self, k=1):
        base = self.n
        self.n += k
        return base


def kernel(*refs):
    it = iter(refs)
    take = lambda n: [next(it) for _ in range(n)]
    tok_h, cot_h, size_s, prefix_s, lens_s, nrm_in = take(6)
    wq_h, wo_h, wu_h, wd_h = take(4)
    bo_h, ig_h, gq_h, go_h, gu_h, gd_h, gn_o = take(7)
    wf_q, wf_o, wf_u, wf_d = take(4)
    own = take(6)
    gat = take(6)
    rcv1 = dict(zip(SCATTER, take(len(SCATTER))))
    rcv2 = dict(zip(SCATTER, take(len(SCATTER))))
    tok, back, bias, a1, qkv, mixed, probs, a2, hid, dup, slope, ps_a, ps_b, gdb = take(14)
    rc = take(3)
    rz = take(3)
    xown, r1, dr1, ybuf, dqkv, ds_s, nst, nbuf, gains, ngrad, nrec, oblk_b, oblk_i = take(13)
    ssem, rsem, lsem = take(3)
    rc = (rc[0], rc[1], rc[2], rc[0])
    rz = (rz[0], rz[1], rz[2], rz[0])
    dt, pb_s = tok, bias
    grad = {D_: gdb, **{k: gat[k] for k in (Q_, K_, V_, O_, U_)}}

    d_at = lax.axis_index("dp")
    t_at = lax.axis_index("tensor")
    x = d_at // 4
    yl = (d_at // 2) % 2
    c = d_at % 2
    z = t_at // 2
    yh = t_at % 2
    y = yh * 2 + yl
    other = 1 - c

    def dev(px, py, pz, pc):
        return {"dp": (px * 2 + py % 2) * 2 + pc, "tensor": pz * 2 + py // 2}

    nr, nl = Counter(), Counter()
    pending, free = [], list(range(N_SEND))[::-1]

    def rcopy(src, dst, to, si, ri):
        return pltpu.make_async_remote_copy(
            src_ref=src, dst_ref=dst, send_sem=ssem.at[si], recv_sem=rsem.at[ri],
            device_id=to, device_id_type=MESH)

    def send(src, dst, to, ri, tag=""):
        si = free.pop()
        cp = rcopy(src, dst, to, si, ri)
        cp.start()
        pending.append((tag, cp, None, si))

    def send_or_local(here, src, dst, to, ri, tag=""):
        si = free.pop()
        cp = rcopy(src, dst, to, si, ri)
        away = jnp.logical_not(here)

        @pl.when(here)
        def _():
            pltpu.make_async_copy(src, dst, rsem.at[ri]).start()

        @pl.when(away)
        def _():
            cp.start()

        pending.append((tag, cp, away, si))

    def send_if(cond, src, dst, to, ri, tag=""):
        si = free.pop()
        cp = rcopy(src, dst, to, si, ri)

        @pl.when(cond)
        def _():
            cp.start()

        pending.append((tag, cp, cond, si))

    def flush(tag=None):
        for item in pending[:]:
            kind, cp, cond, si = item
            if tag is None or kind == tag:
                pending.remove(item)
                free.append(si)
                if cond is None:
                    cp.wait_send()
                else:
                    pl.when(cond)(cp.wait_send)

    def got(dst, ri):
        rcopy(dst, dst, dev(x, y, z, other), 0, ri).wait_recv()

    def load(src, dst):
        cp = pltpu.make_async_copy(src, dst, lsem.at[nl.take()])
        cp.start()
        return cp

    home = c == yh
    my_row = c * 256 + z * 64
    ld_q = load(wq_h, wf_q)
    ld_o = load(wo_h, wf_o)
    ld_t = pltpu.make_async_copy(tok_h, tok, lsem.at[nl.take()])
    ld_c = pltpu.make_async_copy(cot_h, back, lsem.at[nl.take()])
    pl.when(home)(ld_t.start)
    ld_u = load(wu_h, wf_u)
    ld_d = load(wd_h, wf_d)
    pl.when(home)(ld_c.start)

    yp = yh * 2 + (1 - yl)
    peers = [dev(x, y, z, other)]
    for k in (1, 2, 3):
        for cc in (0, 1):
            peers.append(dev((x + k) % 4, y, z, cc))
            peers.append(dev(x, (y + k) % 4, z, cc))
            peers.append(dev(x, y, (z + k) % 4, cc))
            peers.append(dev((x + k) % 4, yp, z, cc))
    barrier = pltpu.get_barrier_semaphore()
    for peer in peers:
        pl.semaphore_signal(barrier, inc=1, device_id=peer, device_id_type=MESH)
    nst[0:4, :] = nrm_in[...].astype(BF).astype(F32)
    nst[4:8, :] = jnp.zeros((4, 128), F32)
    ld_q.wait()
    for j in range(3):
        own[j][...] = wf_q[j].astype(BF)
    ld_o.wait()
    own[O_][...] = wf_o[...].astype(BF)
    pl.when(home)(ld_t.wait)
    pl.semaphore_wait(barrier, len(peers))

    g1_r = {p: nr.take() for p in GATHER}
    g2_r = {p: nr.take(3) for p in GATHER}

    def gather_one(parts):
        for p in parts:
            k, r0, rn, x_first = p
            rows = pl.ds(r0, rn)
            for j in range(4):
                if x_first:
                    to = dev((x + j) % 4, y, z, yh)
                else:
                    to = dev(x, (y + j) % 4, z, yh)
                src, dst = own[k].at[rows], gat[k].at[x, yl, c, rows]
                if j == 0:
                    send_or_local(home, src, dst, to, g1_r[p], "gather")
                else:
                    send(src, dst, to, g1_r[p], "gather")

    r_at = (y + 4 - 2 * c) % 4

    def gather_two(parts):
        for p in parts:
            k, r0, rn, x_first = p
            rows = pl.ds(r0, rn)
            if x_first:
                part = gat[k].at[:, yl, :, rows]

                @pl.when(home)
                def _():
                    got(part, g1_r[p])

                for step in (1, 3):
                    send_if(home, part, part, dev(x, (y + step) % 4, z, c), g2_r[p], "gather")
            else:
                part = gat[k].at[x, :, :, rows]
                got(part, g1_r[p])
                send(part, part, dev((x + 1) % 4, y, z, c), g2_r[p], "gather")
                send(part, part, dev((x + 3) % 4, y, z, c), g2_r[p] + 1, "gather")

    def gather_three(parts):
        for p in parts:
            k, r0, rn, x_first = p
            rows = pl.ds(r0, rn)
            if x_first:
                src_l = 1 - r_at % 2
                got(gat[k].at[:, src_l, :, rows], g2_r[p])
                half = jnp.where((r_at == 0) | (r_at == 3), 1, 0)
                part = gat[k].at[pl.ds(2 * half, 2), src_l, :, rows]
                to = dev(x, (2 * c + 3 - r_at % 2) % 4, z, c)
                send(part, part, to, g2_r[p] + 1, "gather")
            else:
                xm, xp = (x + 3) % 4, (x + 1) % 4
                got(gat[k].at[xm, :, :, rows], g2_r[p])
                part = gat[k].at[xm, 0, :, rows]
                send(part, part, dev(xp, y, z, c), g2_r[p] + 2, "gather")
                got(gat[k].at[xp, :, :, rows], g2_r[p] + 1)
                part = gat[k].at[xp, 1, :, rows]
                send(part, part, dev(xm, y, z, c), g2_r[p] + 2, "gather")

    def gather_end(parts):
        for p in parts:
            k, r0, rn, x_first = p
            rows = pl.ds(r0, rn)
            if x_first:
                @pl.when(r_at >= 2)
                def _():
                    got(gat[k].at[:, r_at % 2, :, rows], g2_r[p] + 1)
            else:
                got(gat[k].at[(x + 2) % 4, :, :, rows], g2_r[p] + 2)

    gather_one(G_QKV)

    tok_r = nr.take(3)

    def share(i, buf):
        send_if(home, buf, buf, dev(x, y, z, other), tok_r + i, "group")

    def shared(i, buf):
        @pl.when(jnp.logical_not(home))
        def _():
            got(buf, tok_r + i)

    norm_r = nr.take()
    pltpu.make_async_copy(nst, nbuf.at[d_at], rsem.at[norm_r]).start()
    for dx in range(4):
        for dl in (0, 1):
            for dc in (0, 1):
                if dx or dl or dc:
                    to = dev((x + dx) % 4, yh * 2 + (yl + dl) % 2, z, (c + dc) % 2)
                    send(nst, nbuf.at[d_at], to, norm_r)
    share(0, tok)
    gather_one(G_OUT)

    ld_u.wait()

    @pl.loop(0, 8)
    def _(i):
        own[U_][ds(i * 16, 16), :] = wf_u[ds(i * 16, 16), :].astype(BF)

    @pl.when(home)
    def _():
        ends = []
        total = prefix_s[0]
        for i in range(16):
            total = total + jnp.where(i < size_s[0], lens_s[0, i], 0)
            ends.append(total)

        def segment(pos):
            seg = jnp.where(pos >= ends[0], 1, 0)
            for i in range(1, 16):
                seg = seg + jnp.where(pos >= ends[i], 1, 0)
            return jnp.where(pos < prefix_s[0], -1, seg)

        row_pos = lax.broadcasted_iota(jnp.int32, (8, ROWS), 1)
        row_seg = segment(row_pos)[0:1, :]
        row_pos = row_pos[0:1, :]

        @pl.loop(0, 8)
        def _(i):
            rows = ds(i * 64, 64)
            pos = lax.broadcasted_iota(jnp.int32, (64, 128), 0) + i * 64
            seg = jnp.concatenate([segment(pos)] * 4, axis=1)
            at = jnp.concatenate([pos] * 4, axis=1)
            linked = (seg == row_seg) | (row_seg < 0)
            live = (at < total) & (row_pos < total) & (row_pos <= at)
            allowed = (linked & live) | (row_pos == at)
            bias[rows, :] = jnp.where(allowed, 0.0, NEG_FILL).astype(BF)

        ld_c.wait()

        @pl.loop(0, 16)
        def _(i):
            rows = ds(i * 32, 32)
            pos = lax.broadcasted_iota(jnp.int32, (32, 128), 0) + i * 32
            keep = jnp.where(pos < total, 1.0, 0.0)
            keep = jnp.concatenate([keep] * 16, axis=1)
            back[rows, :] = (back[rows, :].astype(F32) * keep).astype(BF)

    share(1, bias)
    share(2, back)

    got(nbuf, norm_r)
    for i in range(16):
        gains[:, i * 128:(i + 1) * 128] = nbuf[i]

    gather_two(G_QKV)
    gather_one(G_UP)

    shared(0, tok)

    @pl.loop(0, ROWS // 32)
    def _(i):
        rows = ds(i * 32, 32)
        v = tok[rows, :].astype(F32)
        cen = v - jnp.mean(v, axis=-1, keepdims=True)
        var = jnp.mean(cen * cen, axis=-1, keepdims=True)
        a1[rows, :] = (cen * lax.rsqrt(var + NORM_EPS) * gains[0:1, :] + gains[1:2, :]).astype(BF)

    for i in range(4):
        xown[i * 16:(i + 1) * 16, :] = tok[ds(my_row + i * 16, 16), :]

    ld_d.wait()

    @pl.loop(0, 8)
    def _(i):
        own[D_][ds(i * 128, 128), :] = wf_d[ds(i * 128, 128), :].astype(BF)

    gather_three(G_QKV)
    gather_two(G_OUT)

    def project(j):
        v = dot(a1[...], gat[j][...].reshape(D, 256))
        if j == Q_:
            v = v * SCALE
        qkv[j] = v.astype(BF)

    gather_end(G_QKV)
    project(Q_)
    project(K_)
    project(V_)
    gather_three(G_OUT)
    gather_two(G_UP)
    gather_one(G_DOWN)
    shared(1, bias)

    for h in range(2):
        cols = slice(h * HD, (h + 1) * HD)

        @pl.loop(0, 4)
        def _(i):
            rows = ds(i * 128, 128)
            s = dot(qkv[0, rows, cols], qkv[1, :, cols], NT) + bias[rows, :].astype(F32)
            w = jnp.exp(s - jnp.max(s, axis=-1, keepdims=True))
            p = w / jnp.sum(w, axis=-1, keepdims=True)
            probs[h, rows, :] = p
            mixed[rows, cols] = dot(p.astype(BF), qkv[2, :, cols]).astype(BF)

    rc_r = [nr.take(4) for _ in range(4)]
    rz_r = [nr.take() for _ in range(4)]

    def sum_run(k, ps, compute):
        lo = other * 256

        def combine(j):
            cols = pl.ds(j * 512, 512)
            got(rc[k].at[j], rc_r[k] + j)
            for dz in (2, 1, 3, 0):
                pz = (z + dz) % 4
                rows = ds(c * 256 + pz * 64, 64)
                from_other = rc[k][j, ds(pz * 64, 64), :].astype(F32)
                ps[rows, cols] = (ps[rows, cols].astype(F32) + from_other).astype(BF)
                if dz:
                    send(ps.at[rows, cols], rz[k].at[dz - 1, :, cols], dev(x, y, pz, c),
                         rz_r[k], f"sum{k}")

        for j in range(4):
            cols = pl.ds(j * 512, 512)
            ps[:, cols] = compute(j).astype(BF)
            send(ps.at[ds(lo, 256), cols], rc[k].at[j], dev(x, y, z, other), rc_r[k] + j, f"sum{k}")
            if j:
                combine(j - 1)
        combine(3)

    def sum_wait(k):
        got(rz[k], rz_r[k])

    def sum_rows(k, ps, i):
        rows = ds(i * 16, 16)
        v = ps[ds(my_row + i * 16, 16), :].astype(F32)
        for j in range(3):
            v = v + rz[k][j, rows, :].astype(F32)
        return v

    ag_r = [nr.take(3) for _ in range(2)]
    ac_r = [nr.take() for _ in range(2)]

    def spread_start(k, buf):
        part = buf.at[ds(my_row, 64), :]
        for dz in (2, 1, 3):
            send(part, part, dev(x, y, (z + dz) % 4, c), ag_r[k] + dz - 1)
        send(part, part, dev(x, y, z, other), ac_r[k])

    def spread_pass(k, buf):
        for dz in (1, 3, 2):
            sz = (z + 4 - dz) % 4
            part = buf.at[ds(c * 256 + sz * 64, 64), :]
            got(part, ag_r[k] + dz - 1)
            send(part, part, dev(x, y, z, other), ac_r[k])

    def spread_end(k, buf):
        got(buf.at[ds(other * 256, 256), :], ac_r[k])

    def attn_out(j):
        w = jnp.concatenate([gat[O_][j, a, b] for a in range(2) for b in range(2)], axis=1)
        return dot(mixed[...], w)

    gather_end(G_OUT)
    flush("group")
    sum_run(0, ps_a, attn_out)
    gather_three(G_UP)
    gather_two(G_DOWN)
    sum_wait(0)

    @pl.loop(0, 4)
    def _(i):
        rows = ds(i * 16, 16)
        v = xown[rows, :].astype(F32) + sum_rows(0, ps_a, i)
        r1[rows, :] = v
        cen = v - jnp.mean(v, axis=-1, keepdims=True)
        var = jnp.mean(cen * cen, axis=-1, keepdims=True)
        n = cen * lax.rsqrt(var + NORM_EPS) * gains[2:3, :] + gains[3:4, :]
        a2[ds(my_row + i * 16, 16), :] = n.astype(BF)

    spread_start(0, a2)
    spread_pass(0, a2)
    gather_three(G_DOWN)

    gather_end(G_UP)
    spread_end(0, a2)

    @pl.loop(0, 4)
    def _(i):
        cols = ds(i * 256, 256)
        u = dot(a2[...], gat[U_][:, :, :, :, cols].reshape(D, 256))
        th = jnp.tanh(GELU_K * (u + GELU_C * u * u * u))
        hid[:, cols] = (0.5 * u * (1.0 + th)).astype(BF)
        slope[:, cols] = 0.5 * (1.0 + th) + 0.5 * u * (1.0 - th * th) * (GELU_K * (1.0 + 3.0 * GELU_C * u * u))

    shared(2, back)

    s1_r = {p: nr.take() for p in SCATTER}
    s2_r = {p: nr.take() for p in SCATTER}

    def scatter_one(parts):
        for p in parts:
            k, r0, rn, y_first = p
            rows = pl.ds(r0, rn)
            if y_first:
                for tl in range(2):
                    for tc in range(2):
                        here = home & (yl == tl) & (c == tc)
                        src, dst = grad[k].at[:, tl, tc, rows], rcv1[p].at[y]
                        send_or_local(here, src, dst, dev(x, 2 * c + tl, z, tc), s1_r[p])
            else:
                for dx in (2, 1, 3):
                    px = (x + dx) % 4
                    send(grad[k].at[px, :, :, rows], rcv1[p].at[dx - 1], dev(px, y, z, c), s1_r[p])

    def add_up(parts, out, shape):
        step = 16384 // shape[1]

        @pl.loop(0, shape[0] // step)
        def _(i):
            rows = ds(i * step, step)
            v = parts[0][rows, :].astype(F32)
            for q in parts[1:]:
                v = v + q[rows, :].astype(F32)
            out[rows, :] = v.astype(out.dtype)

    def scatter_two(parts):
        for p in parts:
            scatter_two_of(p)

    def scatter_two_of(p):
        k, r0, rn, y_first = p
        shape = (rn, SHARD[k][1])
        if y_first:
            got(rcv1[p], s1_r[p])
            for dx in (2, 1, 3, 0):
                px = (x + dx) % 4
                out = rcv1[p].at[0, px]
                add_up([rcv1[p].at[sy, px] for sy in range(4)], out, shape)
                if dx == 0:
                    pltpu.make_async_copy(out, rcv2[p].at[x], rsem.at[s2_r[p]]).start()
                else:
                    send(out, rcv2[p].at[x], dev(px, y, z, c), s2_r[p])
        else:
            got(rcv1[p], s1_r[p])
            for a in range(2):
                for b in range(2):
                    out = rcv1[p].at[0, a, b]
                    mine = grad[k].at[x, a, b, pl.ds(r0, rn)]
                    add_up([mine] + [rcv1[p].at[j, a, b] for j in range(3)], out, shape)
                    here = home & (yl == a) & (c == b)
                    send_or_local(here, out, rcv2[p].at[y], dev(x, 2 * c + a, z, b), s2_r[p])

    stage = {Q_: wf_q.at[0], K_: wf_q.at[1], V_: wf_q.at[2], O_: wf_o, U_: wf_u, D_: wf_d}

    def scatter_end(parts):
        for p in parts:
            k, r0, rn, _ = p
            got(rcv2[p], s2_r[p])
            add_up([rcv2[p].at[j] for j in range(4)], stage[k].at[pl.ds(r0, rn)], (rn, SHARD[k][1]))

    @pl.loop(0, 8)
    def _(i):
        v = dot(hid[...], back[:, ds(i * 256, 256)], TN).astype(BF)
        a, b = i // 2, i % 2
        gdb[a, b, 0] = v[:, :128]
        gdb[a, b, 1] = v[:, 128:]

    gather_end(G_DOWN)
    scatter_one(S_DOWN)

    @pl.loop(0, 4)
    def _(i):
        cols = ds(i * 256, 256)
        w = jnp.concatenate([gat[D_][a, b, e, cols, :] for a in range(4) for b in range(2) for e in range(2)], axis=1)
        dup[:, cols] = (dot(back[...], w, NT) * slope[:, cols]).astype(BF)

    def entry(j):
        return dot(dup[...], gat[U_][j].reshape(512, 1024), NT)

    def down(j):
        w = jnp.concatenate([gat[D_][j, a, b] for a in range(2) for b in range(2)], axis=1)
        return dot(hid[...], w)

    flush("sum0")
    sum_run(1, ps_a, entry)
    flush("gather")

    @pl.loop(0, 8)
    def _(i):
        a, b = i // 2, i % 2
        v = dot(a2[:, ds(i * 256, 256)], dup[...], TN).astype(BF)
        gat[U_][a, b, 0] = v[:128]
        gat[U_][a, b, 1] = v[128:]

    scatter_one(S_UP)

    def norm_back(v, dy, gain):
        cen = v - jnp.mean(v, axis=-1, keepdims=True)
        rs = lax.rsqrt(jnp.mean(cen * cen, axis=-1, keepdims=True) + NORM_EPS)
        xh = cen * rs
        e = dy * gain
        dv = rs * (e - jnp.mean(e, axis=-1, keepdims=True) - xh * jnp.mean(e * xh, axis=-1, keepdims=True))
        return dv, jnp.sum(dy * xh, axis=0, keepdims=True), jnp.sum(dy, axis=0, keepdims=True)

    ngrad[...] = jnp.zeros_like(ngrad)
    sum_wait(1)

    @pl.loop(0, 4)
    def _(i):
        rows = ds(i * 16, 16)
        mine = ds(my_row + i * 16, 16)
        dv, dg, db = norm_back(r1[rows, :], sum_rows(1, ps_a, i), gains[2:3, :])
        v = back[mine, :].astype(F32) + dv
        dr1[rows, :] = v
        dt[mine, :] = v.astype(BF)
        ngrad[2:3, :] += dg
        ngrad[3:4, :] += db

    spread_start(1, dt)

    o1_r = [nr.take(8) for _ in range(2)]

    def out_start(k, blk, out):
        part = out.at[ds(my_row, 64), :]
        for dz in (2, 1, 3):
            send(blk, part, dev(x, y, (z + dz) % 4, yh), o1_r[k] + z * 2 + c)
        send_or_local(home, blk, part, dev(x, y, z, yh), o1_r[k] + z * 2 + c)
        y2 = (y + 2) % 4
        send(blk, part, dev(x, y2, z, yh), o1_r[k] + z * 2 + c)

    def out_pass(k, out):
        away = jnp.logical_not(home)
        for sc in range(2):
            part = out.at[ds(sc * 256 + z * 64, 64), :]

            @pl.when(away)
            def _():
                got(part, o1_r[k] + z * 2 + sc)

            for dz in (2, 1, 3):
                send_if(away, part, part, dev(x, y, (z + dz) % 4, c), o1_r[k] + z * 2 + sc)

    def out_end(k, out):
        away = jnp.logical_not(home)
        for sc in range(2):
            for dz in range(4):
                sz = (z + dz) % 4

                def wait_it():
                    got(out.at[ds(sc * 256 + sz * 64, 64), :], o1_r[k] + sz * 2 + sc)

                if dz == 0:
                    pl.when(home)(wait_it)
                else:
                    wait_it()

    sum_run(2, ps_b, down)
    spread_pass(1, dt)
    spread_end(1, dt)

    @pl.loop(0, 2)
    def _(i):
        rows = ds(i * 256, 256)
        w = jnp.concatenate([gat[O_][a, b, e] for a in range(4) for b in range(2) for e in range(2)], axis=1)
        ybuf[rows, :] = dot(dt[rows, :], w, NT).astype(BF)

    for h in range(2):
        cols = slice(h * HD, (h + 1) * HD)

        @pl.loop(0, 4)
        def _(i):
            rows = ds(i * 128, 128)
            p = probs[h, rows, :]
            pb_s[rows, :] = p.astype(BF)
            dp = dot(ybuf[rows, cols], qkv[2, :, cols], NT)
            d_s = (p * (dp - jnp.sum(p * dp, axis=-1, keepdims=True))).astype(BF)
            ds_s[rows, :] = d_s
            dqkv[rows, cols] = dot(d_s, qkv[1, :, cols]).astype(BF)

        dqkv[:, 256 + h * HD:256 + (h + 1) * HD] = dot(ds_s[...], qkv[0, :, cols], TN).astype(BF)
        dqkv[:, 512 + h * HD:512 + (h + 1) * HD] = dot(pb_s[...], ybuf[:, cols], TN).astype(BF)

    def into_norm(j):
        ws = [gat[k][j].reshape(512, 256) for k in range(3)]
        v = dot(dqkv[:, 0:256], ws[0], NT) * SCALE
        v = v + dot(dqkv[:, 256:512], ws[1], NT)
        return v + dot(dqkv[:, 512:768], ws[2], NT)

    flush("sum1")
    sum_run(3, ps_a, into_norm)

    @pl.loop(0, 16)
    def _(i):
        a, b, e = i // 4, (i // 2) % 2, i % 2
        v = dot(a1[:, ds(i * 128, 128)], dqkv[...], TN)
        for k in range(3):
            w = v[:, k * 256:(k + 1) * 256]
            gat[k][a, b, e] = (w * SCALE if k == 0 else w).astype(BF)

    scatter_one(S_QKV)

    @pl.loop(0, 8)
    def _(i):
        v = dot(mixed[...], dt[:, ds(i * 256, 256)], TN).astype(BF)
        gat[O_][i // 2, i % 2, 0] = v[:, :128]
        gat[O_][i // 2, i % 2, 1] = v[:, 128:]

    scatter_one(S_OUT)
    sum_wait(2)

    @pl.loop(0, 4)
    def _(i):
        rows = ds(i * 16, 16)
        oblk_b[rows, :] = (r1[rows, :] + sum_rows(2, ps_b, i)).astype(BF)

    out_start(0, oblk_b, bo_h)
    scatter_two(S_DOWN)
    scatter_two(S_UP)

    sum_wait(3)

    @pl.loop(0, 4)
    def _(i):
        rows = ds(i * 16, 16)
        v = xown[rows, :].astype(F32)
        dv, dg, db = norm_back(v, sum_rows(3, ps_a, i), gains[0:1, :])
        oblk_i[rows, :] = (dr1[rows, :] + dv).astype(BF)
        ngrad[0:1, :] += dg
        ngrad[1:2, :] += db

    out_start(1, oblk_i, ig_h)

    n_r = [nr.take() for _ in range(3)]

    def norm_sum(stage, targets, base):
        for j, to in enumerate(targets):
            send(ngrad, nrec.at[base + j], to, n_r[stage], "norm")
        flush("norm")
        got(nrec.at[pl.ds(base, len(targets))], n_r[stage])
        v = ngrad[...]
        for j in range(len(targets)):
            v = v + nrec[base + j]
        ngrad[...] = v

    norm_sum(0, [dev(x, y, (z + dz) % 4, (c + dc) % 2) for dz in range(4) for dc in range(2) if dz or dc], 0)
    scatter_two(S_QKV)
    scatter_two(S_OUT)
    out_pass(0, bo_h)
    out_pass(1, ig_h)
    norm_sum(1, [dev((x + k) % 4, y, z, c) for k in (1, 2, 3)], 7)
    norm_sum(2, [dev(x, (y + k) % 4, z, c) for k in (1, 2, 3)], 10)
    gn_o[...] = ngrad[:, ds(d_at * 128, 128)]

    def put(src, dst):
        cp = pltpu.make_async_copy(src, dst, lsem.at[nl.take()])
        cp.start()
        return cp

    scatter_end(S_DOWN)
    puts = [put(wf_d, gd_h)]
    scatter_end(S_UP)
    puts.append(put(wf_u, gu_h))
    scatter_end(S_QKV)
    puts.append(put(wf_q, gq_h))
    scatter_end(S_OUT)
    puts.append(put(wf_o, go_h))
    out_end(0, bo_h)
    out_end(1, ig_h)
    for cp in puts:
        cp.wait()
    flush()
    assert nr.n <= N_RECV and nl.n <= N_LOCAL


def run_layer(tokens, cotangent, group_sizes, prefix_lens, solution_lens, norms, w_qkv, w_out, w_up, w_down):
    hbm = pl.BlockSpec(memory_space=pltpu.HBM)
    vmem = pl.BlockSpec(memory_space=pltpu.VMEM)
    smem = pl.BlockSpec(memory_space=pltpu.SMEM)
    buf = lambda s, t=BF: pltpu.VMEM(s, t)
    width = lambda p: (p[2], SHARD[p[0]][1])
    scratch = [buf((3, 128, 256), F32), buf((256, 128), F32), buf((128, 1024), F32), buf((1024, 128), F32)]
    scratch += [buf(s) for s in SHARD]
    scratch += [buf((4, 2, 2) + s) for s in SHARD]
    scratch += [buf(((4, 4) if p[3] else (3, 2, 2)) + width(p)) for p in SCATTER]
    scratch += [buf((4,) + width(p)) for p in SCATTER]
    scratch += [
        buf((ROWS, D)), buf((ROWS, D)), buf((ROWS, ROWS)), buf((ROWS, D)), buf((3, ROWS, 256)),
        buf((ROWS, 256)), buf((2, ROWS, ROWS), F32), buf((ROWS, D)), buf((ROWS, 1024)), buf((ROWS, 1024)),
        buf((ROWS, 1024), F32), buf((ROWS, D)), buf((ROWS, D)), buf((4, 2, 2, 1024, 128)),
    ]
    scratch += [buf((4, 256, 512))] * 3
    scratch += [buf((3, 64, D))] * 3
    scratch += [
        buf((64, D)), buf((64, D), F32), buf((64, D), F32), buf((ROWS, 256)), buf((ROWS, 768)),
        buf((ROWS, ROWS)), buf((8, 128), F32), buf((16, 8, 128), F32), buf((8, D), F32),
        buf((8, D), F32), buf((13, 8, D), F32), buf((64, D)), buf((64, D)),
    ]
    scratch += [pltpu.SemaphoreType.DMA((n,)) for n in (N_SEND, N_RECV, N_LOCAL)]
    out_shape = [
        jax.ShapeDtypeStruct((ROWS, D), BF), jax.ShapeDtypeStruct((ROWS, D), BF),
        jax.ShapeDtypeStruct((3, 128, 256), F32), jax.ShapeDtypeStruct((256, 128), F32),
        jax.ShapeDtypeStruct((128, 1024), F32), jax.ShapeDtypeStruct((1024, 128), F32),
        jax.ShapeDtypeStruct((8, 128), F32),
    ]
    return pl.pallas_call(
        kernel,
        out_shape=out_shape,
        in_specs=[hbm, hbm, smem, smem, smem, vmem, hbm, hbm, hbm, hbm],
        out_specs=[hbm] * 6 + [vmem],
        scratch_shapes=scratch,
        compiler_params=pltpu.CompilerParams(
            collective_id=0, has_side_effects=True, vmem_limit_bytes=63 * 2**20),
    )(tokens, cotangent, group_sizes, prefix_lens, solution_lens, norms, w_qkv, w_out, w_up, w_down)


def adamw(weight, grad_in, first_old, second_old, step_rate, weight_decay):
    first_new = BETA_ONE * first_old + (1.0 - BETA_ONE) * grad_in
    second_new = BETA_TWO * second_old + (1.0 - BETA_TWO) * grad_in * grad_in
    corr_one = 1.0 - BETA_ONE**STEP
    corr_two = 1.0 - BETA_TWO**STEP
    step_dir = first_new / corr_one / (jnp.sqrt(second_new / corr_two) + ADAM_EPS)
    weight_new = weight - step_rate * (step_dir + weight_decay * weight)
    return (grad_in, first_new, second_new, weight_new, weight_new.astype(jnp.bfloat16))


RATES = ((RATE_QKV, DECAY_RATE), (RATE_OUT, DECAY_RATE), (RATE_UP, DECAY_RATE), (RATE_DOWN, DECAY_RATE),
         (RATE_NORMS, 0.0))


def finish_kernel(bo, ig, *refs):
    ins, outs = refs[:20], refs[20:]
    outs[0][...] = bo[...]
    outs[1][...] = ig[...].astype(F32)
    for k, (rate, decay) in enumerate(RATES):
        w, g, m, v = (r[...] for r in ins[4 * k:4 * k + 4])
        if k == 4:
            g = g[0:4, :]
        for o, r in zip(outs[2 + 5 * k:7 + 5 * k], adamw(w, g, m, v, rate, decay)):
            o[...] = r


def finish(block_out, input_grad, sets):
    steps = 8
    whole = lambda s: pl.BlockSpec(s, lambda i: (0, 0))
    blocks = [
        pl.BlockSpec((3, 128 // steps, 256), lambda i: (0, i, 0)),
        pl.BlockSpec((256 // steps, 128), lambda i: (i, 0)),
        pl.BlockSpec((128 // steps, 1024), lambda i: (i, 0)),
        pl.BlockSpec((1024 // steps, 128), lambda i: (i, 0)),
        whole((4, 128)),
    ]
    rows = pl.BlockSpec((ROWS // steps, D), lambda i: (i, 0))
    in_specs, out_specs = [rows, rows], [rows, rows]
    out_shape = [jax.ShapeDtypeStruct((ROWS, D), BF), jax.ShapeDtypeStruct((ROWS, D), F32)]
    args = [block_out, input_grad]
    for spec, (w, g, m, v) in zip(blocks, sets):
        args += [w, g, m, v]
        in_specs += [spec, whole((8, 128)) if g.shape == (8, 128) else spec, spec, spec]
        out_specs += [spec] * 5
        out_shape += [jax.ShapeDtypeStruct(w.shape, F32)] * 4 + [jax.ShapeDtypeStruct(w.shape, BF)]
    return pl.pallas_call(
        finish_kernel, grid=(steps,), out_shape=out_shape, in_specs=in_specs, out_specs=out_specs,
        compiler_params=pltpu.CompilerParams(vmem_limit_bytes=63 * 2**20),
    )(*args)


def per_device(
    tokens, cotangent, group_sizes, prefix_lens, solution_lens,
    w_qkv, w_out, w_up, w_down, norms,
    first_qkv, second_qkv, first_out, second_out,
    first_up, second_up, first_down, second_down, first_norms, second_norms,
):
    block_out, input_grad, grad_qkv, grad_out, grad_up, grad_down, grad_norms = run_layer(
        tokens, cotangent, group_sizes, prefix_lens, solution_lens, norms, w_qkv, w_out, w_up, w_down)
    sets = (
        (w_qkv, grad_qkv, first_qkv, second_qkv),
        (w_out, grad_out, first_out, second_out),
        (w_up, grad_up, first_up, second_up),
        (w_down, grad_down, first_down, second_down),
        (norms, grad_norms, first_norms, second_norms),
    )
    return tuple(finish(block_out, input_grad, sets))


def solution(mesh):
    row, mat = P("dp", None), P("tensor", "dp")
    qkv, up, nrm = P(None, "dp", "tensor"), P("dp", "tensor"), P(None, "dp")
    return jax.shard_map(
        per_device,
        mesh=mesh,
        in_specs=(row, row, P("dp"), P("dp"), row, qkv, mat, up, mat, nrm,
                  qkv, qkv, mat, mat, up, up, mat, mat, nrm, nrm),
        out_specs=(row, row) + (qkv,) * 5 + (mat,) * 5 + (up,) * 5 + (mat,) * 5 + (nrm,) * 5,
        check_vma=False,
    )
```

```python
import functools

import jax
import jax.numpy as jnp
from jax import lax
from jax.experimental import pallas as pl
from jax.experimental.pallas import tpu as pltpu
from jax.sharding import PartitionSpec as P

HD = 128
STEP = 5
ROWS = 512
D = 2048
NEG_FILL = -1e30
BETA_ONE = 0.5
BETA_TWO = 0.5
ADAM_EPS = 1e-08
NORM_EPS = 1e-05
DECAY_RATE = 0.1
RATE_QKV = 0.02
RATE_OUT = 0.15
RATE_UP = 0.02
RATE_DOWN = 0.01
RATE_NORMS = 0.3
SCALE = HD ** (-0.5)
GELU_K = 0.7978845608028654
GELU_C = 0.044715

BF = jnp.bfloat16
F32 = jnp.float32
MESH = pl.DeviceIdType.MESH
NT = (((1,), (1,)), ((), ()))
TN = (((0,), (0,)), ((), ()))
NN = (((1,), (0,)), ((), ()))

SHARD = ((128, 256), (128, 256), (128, 256), (256, 128), (128, 1024), (1024, 128))
Q_, K_, V_, O_, U_, D_ = range(6)
G_QK = ((Q_, 0, 64, True), (Q_, 64, 64, False), (K_, 0, 64, True), (K_, 64, 64, False))
G_V = ((V_, 0, 64, True), (V_, 64, 64, False))
G_OUT = ((O_, 0, 128, True), (O_, 128, 128, False))
G_UP = ((U_, 0, 64, True), (U_, 64, 64, False))
G_DOWN = ((D_, 0, 512, True), (D_, 512, 512, False))
GATHER = G_QK + G_V + G_OUT + G_UP + G_DOWN
S_DOWN = ((D_, 0, 512, True), (D_, 512, 512, False))
S_UP = ((U_, 0, 64, True), (U_, 64, 64, False))
S_QKV = ((Q_, 0, 128, True), (K_, 0, 128, False), (V_, 0, 64, True), (V_, 64, 64, False))
S_OUT = ((O_, 0, 128, True), (O_, 128, 128, False))
SCATTER = S_DOWN + S_UP + S_QKV + S_OUT


def dot(a, b, dims=NN):
    return lax.dot_general(a, b, dims, preferred_element_type=F32)


def ds(start, size, mult=None):
    if not isinstance(start, int):
        start = pl.multiple_of(start, mult or size)
    return pl.ds(start, size)


F_SUM, F_SPREAD, F_OUT = 0, 1, 1
N_SEND = 200
N_RECV = 180
N_LOCAL = 16


class Counter:
    def __init__(self):
        self.n = 0

    def take(self, k=1):
        base = self.n
        self.n += k
        return base


def kernel(*refs):
    it = iter(refs)
    take = lambda n: [next(it) for _ in range(n)]
    tok_h, cot_h, size_s, prefix_s, lens_s, nrm_in = take(6)
    wq_h, wo_h, wu_h, wd_h = take(4)
    bo_h, ig_h, gq_h, go_h, gu_h, gd_h, gn_o = take(7)
    wf_q, wf_o, wf_u, wf_d = take(4)
    own = take(6)
    gat = take(6)
    rcv1 = dict(zip(SCATTER, take(len(SCATTER))))
    rcv2 = dict(zip(SCATTER, take(len(SCATTER))))
    tok, back, bias, a1, qkv, mixed, probs, a2, hid, dup, slope, ps_a, ps_b, gdb = take(14)
    rc = take(3)
    rz = take(3)
    relay = take(3)
    xown, r1, dr1, ybuf, dqkv, ds_s, nst, nbuf, gains, ngrad, nrec, oblk_b, oblk_i = take(13)
    ssem, rsem, lsem = take(3)
    rc = (rc[0], rc[1], rc[2], rc[0])
    rz = (rz[0], rz[1], rz[2], rz[0])
    relay = (relay[0], relay[1], relay[2], relay[0])
    dt, pb_s = tok, bias
    grad = {D_: gdb, **{k: gat[k] for k in (Q_, K_, V_, O_, U_)}}

    d_at = lax.axis_index("dp")
    t_at = lax.axis_index("tensor")
    x = d_at // 4
    yl = (d_at // 2) % 2
    c = d_at % 2
    z = t_at // 2
    yh = t_at % 2
    y = yh * 2 + yl
    other = 1 - c

    def dev(px, py, pz, pc):
        return {"dp": (px * 2 + py % 2) * 2 + pc, "tensor": pz * 2 + py // 2}

    nr, nl = Counter(), Counter()
    pending, free = [], list(range(N_SEND))[::-1]

    def rcopy(src, dst, to, si, ri):
        return pltpu.make_async_remote_copy(
            src_ref=src, dst_ref=dst, send_sem=ssem.at[si], recv_sem=rsem.at[ri],
            device_id=to, device_id_type=MESH)

    def send(src, dst, to, ri, tag=""):
        si = free.pop()
        cp = rcopy(src, dst, to, si, ri)
        cp.start()
        pending.append((tag, cp, None, si))

    def send_or_local(here, src, dst, to, ri, tag=""):
        si = free.pop()
        cp = rcopy(src, dst, to, si, ri)
        away = jnp.logical_not(here)

        @pl.when(here)
        def _():
            pltpu.make_async_copy(src, dst, rsem.at[ri]).start()

        @pl.when(away)
        def _():
            cp.start()

        pending.append((tag, cp, away, si))

    def send_if(cond, src, dst, to, ri, tag=""):
        si = free.pop()
        cp = rcopy(src, dst, to, si, ri)

        @pl.when(cond)
        def _():
            cp.start()

        pending.append((tag, cp, cond, si))

    def flush(tag=None):
        for item in pending[:]:
            kind, cp, cond, si = item
            if tag is None or kind == tag:
                pending.remove(item)
                free.append(si)
                if cond is None:
                    cp.wait_send()
                else:
                    pl.when(cond)(cp.wait_send)

    def got(dst, ri):
        rcopy(dst, dst, dev(x, y, z, other), 0, ri).wait_recv()

    def load(src, dst):
        cp = pltpu.make_async_copy(src, dst, lsem.at[nl.take()])
        cp.start()
        return cp

    home = c == yh
    my_row = c * 256 + z * 64
    ld_q = load(wq_h, wf_q)
    ld_o = load(wo_h, wf_o)
    ld_t = pltpu.make_async_copy(tok_h, tok, lsem.at[nl.take()])
    ld_c = pltpu.make_async_copy(cot_h, back, lsem.at[nl.take()])
    pl.when(home)(ld_t.start)
    ld_u = load(wu_h, wf_u)
    ld_d = load(wd_h, wf_d)
    pl.when(home)(ld_c.start)

    yp = yh * 2 + (1 - yl)
    peers = [dev(x, y, z, other)]
    for k in (1, 2, 3):
        for cc in (0, 1):
            peers.append(dev((x + k) % 4, y, z, cc))
            peers.append(dev(x, (y + k) % 4, z, cc))
            peers.append(dev(x, y, (z + k) % 4, cc))
            peers.append(dev((x + k) % 4, yp, z, cc))
    barrier = pltpu.get_barrier_semaphore()
    for peer in peers:
        pl.semaphore_signal(barrier, inc=1, device_id=peer, device_id_type=MESH)
    nst[0:4, :] = nrm_in[...].astype(BF).astype(F32)
    nst[4:8, :] = jnp.zeros((4, 128), F32)
    ld_q.wait()
    for j in range(3):
        own[j][...] = wf_q[j].astype(BF)
    ld_o.wait()
    own[O_][...] = wf_o[...].astype(BF)
    pl.when(home)(ld_t.wait)
    pl.semaphore_wait(barrier, len(peers))

    g1_r = {p: nr.take() for p in GATHER}
    g2_r = {p: nr.take(3) for p in GATHER}

    def gather_one(parts):
        for p in parts:
            k, r0, rn, x_first = p
            rows = pl.ds(r0, rn)
            for j in range(4):
                if x_first:
                    to = dev((x + j) % 4, y, z, yh)
                else:
                    to = dev(x, (y + j) % 4, z, yh)
                src, dst = own[k].at[rows], gat[k].at[x, yl, c, rows]
                if j == 0:
                    send_or_local(home, src, dst, to, g1_r[p], "gather")
                else:
                    send(src, dst, to, g1_r[p], "gather")

    r_at = (y + 4 - 2 * c) % 4

    def gather_two(parts):
        for p in parts:
            k, r0, rn, x_first = p
            rows = pl.ds(r0, rn)
            if x_first:
                part = gat[k].at[:, yl, :, rows]

                @pl.when(home)
                def _():
                    got(part, g1_r[p])

                for step in (1, 3):
                    send_if(home, part, part, dev(x, (y + step) % 4, z, c), g2_r[p], "gather")
            else:
                part = gat[k].at[x, :, :, rows]
                got(part, g1_r[p])
                send(part, part, dev((x + 1) % 4, y, z, c), g2_r[p], "gather")
                send(part, part, dev((x + 3) % 4, y, z, c), g2_r[p] + 1, "gather")

    def gather_three(parts):
        for p in parts:
            k, r0, rn, x_first = p
            rows = pl.ds(r0, rn)
            if x_first:
                src_l = 1 - r_at % 2
                got(gat[k].at[:, src_l, :, rows], g2_r[p])
                half = jnp.where((r_at == 0) | (r_at == 3), 1, 0)
                part = gat[k].at[pl.ds(2 * half, 2), src_l, :, rows]
                to = dev(x, (2 * c + 3 - r_at % 2) % 4, z, c)
                send(part, part, to, g2_r[p] + 1, "gather")
            else:
                xm, xp = (x + 3) % 4, (x + 1) % 4
                got(gat[k].at[xm, :, :, rows], g2_r[p])
                part = gat[k].at[xm, 0, :, rows]
                send(part, part, dev(xp, y, z, c), g2_r[p] + 2, "gather")
                got(gat[k].at[xp, :, :, rows], g2_r[p] + 1)
                part = gat[k].at[xp, 1, :, rows]
                send(part, part, dev(xm, y, z, c), g2_r[p] + 2, "gather")

    def gather_end(parts):
        for p in parts:
            k, r0, rn, x_first = p
            rows = pl.ds(r0, rn)
            if x_first:
                @pl.when(r_at >= 2)
                def _():
                    got(gat[k].at[:, r_at % 2, :, rows], g2_r[p] + 1)
            else:
                got(gat[k].at[(x + 2) % 4, :, :, rows], g2_r[p] + 2)

    gather_one(G_QK)
    gather_one(G_V)

    tok_r = nr.take(3)

    def share(i, buf):
        send_if(home, buf, buf, dev(x, y, z, other), tok_r + i, "group")

    def shared(i, buf):
        @pl.when(jnp.logical_not(home))
        def _():
            got(buf, tok_r + i)

    norm_r = nr.take()
    pltpu.make_async_copy(nst, nbuf.at[d_at], rsem.at[norm_r]).start()
    for dx in range(4):
        for dl in (0, 1):
            for dc in (0, 1):
                if dx or dl or dc:
                    to = dev((x + dx) % 4, yh * 2 + (yl + dl) % 2, z, (c + dc) % 2)
                    send(nst, nbuf.at[d_at], to, norm_r)
    share(0, tok)
    gather_one(G_OUT)

    ld_u.wait()

    @pl.loop(0, 8)
    def _(i):
        own[U_][ds(i * 16, 16), :] = wf_u[ds(i * 16, 16), :].astype(BF)

    @pl.when(home)
    def _():
        ends = []
        total = prefix_s[0]
        for i in range(16):
            total = total + jnp.where(i < size_s[0], lens_s[0, i], 0)
            ends.append(total)

        def segment(pos):
            seg = jnp.where(pos >= ends[0], 1, 0)
            for i in range(1, 16):
                seg = seg + jnp.where(pos >= ends[i], 1, 0)
            return jnp.where(pos < prefix_s[0], -1, seg)

        row_pos = lax.broadcasted_iota(jnp.int32, (8, ROWS), 1)
        row_seg = segment(row_pos)[0:1, :]
        row_pos = row_pos[0:1, :]

        @pl.loop(0, 8)
        def _(i):
            rows = ds(i * 64, 64)
            pos = lax.broadcasted_iota(jnp.int32, (64, 128), 0) + i * 64
            seg = jnp.concatenate([segment(pos)] * 4, axis=1)
            at = jnp.concatenate([pos] * 4, axis=1)
            linked = (seg == row_seg) | (row_seg < 0)
            live = (at < total) & (row_pos < total) & (row_pos <= at)
            allowed = (linked & live) | (row_pos == at)
            bias[rows, :] = jnp.where(allowed, 0.0, NEG_FILL).astype(BF)

        ld_c.wait()

        @pl.loop(0, 16)
        def _(i):
            rows = ds(i * 32, 32)
            pos = lax.broadcasted_iota(jnp.int32, (32, 128), 0) + i * 32
            keep = jnp.where(pos < total, 1.0, 0.0)
            keep = jnp.concatenate([keep] * 16, axis=1)
            back[rows, :] = (back[rows, :].astype(F32) * keep).astype(BF)

    share(1, bias)
    share(2, back)

    got(nbuf, norm_r)
    for i in range(16):
        gains[:, i * 128:(i + 1) * 128] = nbuf[i]

    gather_two(G_QK)
    gather_two(G_V)
    gather_one(G_UP)

    shared(0, tok)

    @pl.loop(0, ROWS // 32)
    def _(i):
        rows = ds(i * 32, 32)
        v = tok[rows, :].astype(F32)
        cen = v - jnp.mean(v, axis=-1, keepdims=True)
        var = jnp.mean(cen * cen, axis=-1, keepdims=True)
        a1[rows, :] = (cen * lax.rsqrt(var + NORM_EPS) * gains[0:1, :] + gains[1:2, :]).astype(BF)

    for i in range(4):
        xown[i * 16:(i + 1) * 16, :] = tok[ds(my_row + i * 16, 16), :]

    ld_d.wait()

    @pl.loop(0, 8)
    def _(i):
        own[D_][ds(i * 128, 128), :] = wf_d[ds(i * 128, 128), :].astype(BF)

    gather_three(G_QK)
    gather_three(G_V)
    gather_two(G_OUT)

    def project(j):
        v = dot(a1[...], gat[j][...].reshape(D, 256))
        if j == Q_:
            v = v * SCALE
        qkv[j] = v.astype(BF)

    gather_end(G_QK)
    gather_end(G_V)
    project(Q_)
    project(K_)
    project(V_)
    gather_three(G_OUT)
    gather_two(G_UP)
    gather_one(G_DOWN)
    shared(1, bias)

    for h in range(2):
        cols = slice(h * HD, (h + 1) * HD)

        @pl.loop(0, 4)
        def _(i):
            rows = ds(i * 128, 128)
            s = dot(qkv[0, rows, cols], qkv[1, :, cols], NT) + bias[rows, :].astype(F32)
            w = jnp.exp(s - jnp.max(s, axis=-1, keepdims=True))
            probs[h, rows, :] = w / jnp.sum(w, axis=-1, keepdims=True)

    for h in range(2):
        cols = slice(h * HD, (h + 1) * HD)
        mixed[:, cols] = dot(probs[h].astype(BF), qkv[2, :, cols]).astype(BF)

    rc_r = [nr.take(4) for _ in range(4)]
    rz_r = [nr.take() for _ in range(4)]
    rl_r = [nr.take(4) for _ in range(4)]

    def z_block(dz):
        return c * 256 + (z + dz) % 4 * 64

    def sum_combine(k, ps, j):
        cols = pl.ds(j * 512, 512)
        got(rc[k].at[j], rc_r[k] + j)
        for dz in (2, 1, 3, 0):
            rows = ds(z_block(dz), 64)
            from_other = rc[k][j, ds((z + dz) % 4 * 64, 64), :].astype(F32)
            ps[rows, cols] = (ps[rows, cols].astype(F32) + from_other).astype(BF)

    def sum_relay(k, ps, j):
        cols = pl.ds(j * 512, 512)
        if not F_SUM:
            for dz in (2, 1, 3):
                send(ps.at[ds(z_block(dz), 64), cols], rz[k].at[dz - 1, :, cols], dev(x, y, (z + dz) % 4, c),
                     rz_r[k], f"sum{k}")
            return
        for half, step in ((0, 1), (1, 3)):
            send(ps.at[ds(z_block(2) + half * 32, 32), cols], relay[k].at[j, half],
                 dev(x, y, (z + step) % 4, c), rl_r[k] + j, f"sum{k}")

    def sum_pass(k, ps, j):
        if not F_SUM:
            return
        cols = pl.ds(j * 512, 512)
        got(relay[k].at[j], rl_r[k] + j)
        for half, step in ((0, 1), (1, 3)):
            rows = ds(z_block(step) + half * 32, 32)
            ps[rows, cols] = (ps[rows, cols].astype(F32) + relay[k][j, half].astype(F32)).astype(BF)
            send(ps.at[ds(z_block(step), 64), cols], rz[k].at[half, :, cols],
                 dev(x, y, (z + step) % 4, c), rz_r[k], f"sum{k}")

    def sum_part(k, ps, compute, j):
        cols = pl.ds(j * 512, 512)
        ps[:, cols] = compute(j).astype(BF)
        half = ps.at[ds(other * 256, 256), cols]
        send(half, rc[k].at[j], dev(x, y, z, other), rc_r[k] + j, f"sum{k}")

    def sum_run(k, ps, compute):
        for j in range(7):
            if j < 4:
                sum_part(k, ps, compute, j)
            if 1 <= j < 5:
                sum_combine(k, ps, j - 1)
                sum_relay(k, ps, j - 1)
            if 2 <= j < 6:
                sum_pass(k, ps, j - 2)

    def sum_wait(k):
        got(rz[k], rz_r[k])

    def sum_rows(k, ps, i):
        rows = ds(i * 16, 16)
        v = ps[ds(my_row + i * 16, 16), :].astype(F32)
        for j in range(2 if F_SUM else 3):
            v = v + rz[k][j, rows, :].astype(F32)
        return v

    ag_r = [nr.take(3) for _ in range(2)]
    ac_r = [nr.take() for _ in range(2)]

    def spread_start(k, buf):
        part = buf.at[ds(my_row, 64), :]
        for half, step in ((0, 1), (1, 3)):
            send(part, part, dev(x, y, (z + step) % 4, c), ag_r[k] + half)
        if not F_SPREAD:
            send(part, part, dev(x, y, (z + 2) % 4, c), ag_r[k] + 2)
        send(part, part, dev(x, y, z, other), ac_r[k])

    def spread_pass(k, buf):
        base = c * 256
        for half, step in ((0, 1), (1, 3)):
            at = base + (z + 4 - step) % 4 * 64
            part = buf.at[ds(at, 64), :]
            got(part, ag_r[k] + half)
            piece = buf.at[ds(at + half * 32, 32), :]
            if F_SPREAD:
                send(piece, piece, dev(x, y, (z + step) % 4, c), ag_r[k] + 2)
            send(part, part, dev(x, y, z, other), ac_r[k])
        part = buf.at[ds(base + (z + 2) % 4 * 64, 64), :]
        got(part, ag_r[k] + 2)
        send(part, part, dev(x, y, z, other), ac_r[k])

    def spread_end(k, buf):
        got(buf.at[ds(other * 256, 256), :], ac_r[k])

    def attn_out(j):
        w = jnp.concatenate([gat[O_][j, a, b] for a in range(2) for b in range(2)], axis=1)
        return dot(mixed[...], w)

    gather_end(G_OUT)
    flush("group")
    sum_run(0, ps_a, attn_out)
    gather_three(G_UP)
    gather_two(G_DOWN)
    sum_wait(0)

    @pl.loop(0, 4)
    def _(i):
        rows = ds(i * 16, 16)
        v = xown[rows, :].astype(F32) + sum_rows(0, ps_a, i)
        r1[rows, :] = v
        cen = v - jnp.mean(v, axis=-1, keepdims=True)
        var = jnp.mean(cen * cen, axis=-1, keepdims=True)
        n = cen * lax.rsqrt(var + NORM_EPS) * gains[2:3, :] + gains[3:4, :]
        a2[ds(my_row + i * 16, 16), :] = n.astype(BF)

    spread_start(0, a2)
    spread_pass(0, a2)
    gather_three(G_DOWN)

    gather_end(G_UP)
    spread_end(0, a2)

    @pl.loop(0, 4)
    def _(i):
        cols = ds(i * 256, 256)
        u = dot(a2[...], gat[U_][:, :, :, :, cols].reshape(D, 256))
        th = jnp.tanh(GELU_K * (u + GELU_C * u * u * u))
        hid[:, cols] = (0.5 * u * (1.0 + th)).astype(BF)
        slope[:, cols] = 0.5 * (1.0 + th) + 0.5 * u * (1.0 - th * th) * (GELU_K * (1.0 + 3.0 * GELU_C * u * u))

    shared(2, back)

    s1_r = {p: nr.take() for p in SCATTER}
    s2_r = {p: nr.take() for p in SCATTER}

    def scatter_one(parts):
        for p in parts:
            k, r0, rn, y_first = p
            rows = pl.ds(r0, rn)
            if y_first:
                for tl in range(2):
                    for tc in range(2):
                        here = home & (yl == tl) & (c == tc)
                        src, dst = grad[k].at[:, tl, tc, rows], rcv1[p].at[y]
                        send_or_local(here, src, dst, dev(x, 2 * c + tl, z, tc), s1_r[p])
            else:
                for dx in (2, 1, 3):
                    px = (x + dx) % 4
                    send(grad[k].at[px, :, :, rows], rcv1[p].at[dx - 1], dev(px, y, z, c), s1_r[p])

    def add_up(parts, out, shape):
        step = 16384 // shape[1]

        @pl.loop(0, shape[0] // step)
        def _(i):
            rows = ds(i * step, step)
            v = parts[0][rows, :].astype(F32)
            for q in parts[1:]:
                v = v + q[rows, :].astype(F32)
            out[rows, :] = v.astype(out.dtype)

    def scatter_two(parts):
        for p in parts:
            scatter_two_of(p)

    def scatter_two_of(p):
        k, r0, rn, y_first = p
        shape = (rn, SHARD[k][1])
        if y_first:
            got(rcv1[p], s1_r[p])
            for dx in (2, 1, 3, 0):
                px = (x + dx) % 4
                out = rcv1[p].at[0, px]
                add_up([rcv1[p].at[sy, px] for sy in range(4)], out, shape)
                if dx == 0:
                    pltpu.make_async_copy(out, rcv2[p].at[x], rsem.at[s2_r[p]]).start()
                else:
                    send(out, rcv2[p].at[x], dev(px, y, z, c), s2_r[p])
        else:
            got(rcv1[p], s1_r[p])
            for a in range(2):
                for b in range(2):
                    out = rcv1[p].at[0, a, b]
                    mine = grad[k].at[x, a, b, pl.ds(r0, rn)]
                    add_up([mine] + [rcv1[p].at[j, a, b] for j in range(3)], out, shape)
                    here = home & (yl == a) & (c == b)
                    send_or_local(here, out, rcv2[p].at[y], dev(x, 2 * c + a, z, b), s2_r[p])

    stage = {Q_: wf_q.at[0], K_: wf_q.at[1], V_: wf_q.at[2], O_: wf_o, U_: wf_u, D_: wf_d}

    def scatter_end(parts):
        for p in parts:
            k, r0, rn, _ = p
            got(rcv2[p], s2_r[p])
            add_up([rcv2[p].at[j] for j in range(4)], stage[k].at[pl.ds(r0, rn)], (rn, SHARD[k][1]))

    @pl.loop(0, 4)
    def _(i):
        v = dot(hid[...], back[:, ds(i * 512, 512)], TN).astype(BF)
        for n in range(4):
            gdb[i, n // 2, n % 2] = v[:, n * 128:(n + 1) * 128]

    gather_end(G_DOWN)
    scatter_one(S_DOWN)

    @pl.loop(0, 4)
    def _(i):
        cols = ds(i * 256, 256)
        w = jnp.concatenate([gat[D_][a, b, e, cols, :] for a in range(4) for b in range(2) for e in range(2)], axis=1)
        dup[:, cols] = (dot(back[...], w, NT) * slope[:, cols]).astype(BF)

    def entry(j):
        return dot(dup[...], gat[U_][j].reshape(512, 1024), NT)

    def down(j):
        w = jnp.concatenate([gat[D_][j, a, b] for a in range(2) for b in range(2)], axis=1)
        return dot(hid[...], w)

    flush("sum0")
    sum_run(1, ps_a, entry)
    flush("gather")

    @pl.loop(0, 4)
    def _(i):
        v = dot(a2[:, ds(i * 512, 512)], dup[...], TN).astype(BF)
        for n in range(4):
            gat[U_][i, n // 2, n % 2] = v[n * 128:(n + 1) * 128]

    scatter_one(S_UP)

    def norm_back(v, dy, gain):
        cen = v - jnp.mean(v, axis=-1, keepdims=True)
        rs = lax.rsqrt(jnp.mean(cen * cen, axis=-1, keepdims=True) + NORM_EPS)
        xh = cen * rs
        e = dy * gain
        dv = rs * (e - jnp.mean(e, axis=-1, keepdims=True) - xh * jnp.mean(e * xh, axis=-1, keepdims=True))
        return dv, jnp.sum(dy * xh, axis=0, keepdims=True), jnp.sum(dy, axis=0, keepdims=True)

    ngrad[...] = jnp.zeros_like(ngrad)
    sum_wait(1)

    @pl.loop(0, 4)
    def _(i):
        rows = ds(i * 16, 16)
        mine = ds(my_row + i * 16, 16)
        dv, dg, db = norm_back(r1[rows, :], sum_rows(1, ps_a, i), gains[2:3, :])
        v = back[mine, :].astype(F32) + dv
        dr1[rows, :] = v
        dt[mine, :] = v.astype(BF)
        ngrad[2:3, :] += dg
        ngrad[3:4, :] += db

    spread_start(1, dt)

    o1_r = [nr.take(8) for _ in range(2)]

    def out_rows(out, sz, sc, first=0, rows=64):
        return out.at[ds(sc * 256 + sz % 4 * 64 + first, rows), :]

    def out_start(k, blk, out):
        part = out.at[ds(my_row, 64), :]
        send(blk, part, dev(x, (y + 2) % 4, z, yh), o1_r[k] + c)
        for half, step in ((0, 1), (1, 3)):
            send(blk, part, dev(x, y, (z + step) % 4, yh), o1_r[k] + 2 + half * 2 + c)
        if not F_OUT:
            send(blk, part, dev(x, y, (z + 2) % 4, yh), o1_r[k] + 6 + c)
        send_or_local(home, blk, part, dev(x, y, z, yh), o1_r[k] + c)

    def out_two(k, out):
        for sc in range(2):
            part = out_rows(out, z, sc)
            got(part, o1_r[k] + sc)
            for half, step in ((0, 1), (1, 3)):
                send_if(jnp.logical_not(home), part, part, dev(x, y, (z + step) % 4, c),
                        o1_r[k] + 2 + half * 2 + sc)
            if not F_OUT:
                send_if(jnp.logical_not(home), part, part, dev(x, y, (z + 2) % 4, c), o1_r[k] + 6 + sc)

    def out_three(k, out):
        for sc in range(2):
            for half, step in ((0, 1), (1, 3)):
                got(out_rows(out, z + 4 - step, sc), o1_r[k] + 2 + half * 2 + sc)
                if not F_OUT:
                    continue
                piece = out_rows(out, z + 4 - step, sc, half * 32, 32)
                send(piece, piece, dev(x, y, (z + step) % 4, c), o1_r[k] + 6 + sc)

    def out_end(k, out):
        for sc in range(2):
            got(out_rows(out, z + 2, sc), o1_r[k] + 6 + sc)

    for j in range(4):
        sum_part(2, ps_b, down, j)
    spread_pass(1, dt)
    for j in range(4):
        sum_combine(2, ps_b, j)
        sum_relay(2, ps_b, j)
    spread_end(1, dt)

    @pl.loop(0, 2)
    def _(i):
        rows = ds(i * 256, 256)
        w = jnp.concatenate([gat[O_][a, b, e] for a in range(4) for b in range(2) for e in range(2)], axis=1)
        ybuf[rows, :] = dot(dt[rows, :], w, NT).astype(BF)

    for h in range(2):
        cols = slice(h * HD, (h + 1) * HD)

        @pl.loop(0, 4)
        def _(i):
            rows = ds(i * 128, 128)
            p = probs[h, rows, :]
            pb_s[rows, :] = p.astype(BF)
            dp = dot(ybuf[rows, cols], qkv[2, :, cols], NT)
            d_s = (p * (dp - jnp.sum(p * dp, axis=-1, keepdims=True))).astype(BF)
            ds_s[rows, :] = d_s
            dqkv[rows, cols] = dot(d_s, qkv[1, :, cols]).astype(BF)

        dqkv[:, 256 + h * HD:256 + (h + 1) * HD] = dot(ds_s[...], qkv[0, :, cols], TN).astype(BF)
        dqkv[:, 512 + h * HD:512 + (h + 1) * HD] = dot(pb_s[...], ybuf[:, cols], TN).astype(BF)

    def into_norm(j):
        ws = [gat[k][j].reshape(512, 256) for k in range(3)]
        v = dot(dqkv[:, 0:256], ws[0], NT) * SCALE
        v = v + dot(dqkv[:, 256:512], ws[1], NT)
        return v + dot(dqkv[:, 512:768], ws[2], NT)

    flush("sum1")
    for j in range(4):
        sum_pass(2, ps_b, j)
    sum_run(3, ps_a, into_norm)
    sum_wait(2)

    @pl.loop(0, 4)
    def _(i):
        rows = ds(i * 16, 16)
        oblk_b[rows, :] = (r1[rows, :] + sum_rows(2, ps_b, i)).astype(BF)

    out_start(0, oblk_b, bo_h)

    @pl.loop(0, 4)
    def _(i):
        v = dot(mixed[...], dt[:, ds(i * 512, 512)], TN).astype(BF)
        for n in range(4):
            gat[O_][i, n // 2, n % 2] = v[:, n * 128:(n + 1) * 128]

    scatter_one(S_OUT)

    @pl.loop(0, 8)
    def _(i):
        v = dot(a1[:, ds(i * 256, 256)], dqkv[...], TN)
        for k in range(3):
            w = v[:, k * 256:(k + 1) * 256]
            w = (w * SCALE if k == 0 else w).astype(BF)
            gat[k][i // 2, i % 2, 0] = w[:128]
            gat[k][i // 2, i % 2, 1] = w[128:]

    scatter_one(S_QKV)
    out_two(0, bo_h)

    sum_wait(3)

    @pl.loop(0, 4)
    def _(i):
        rows = ds(i * 16, 16)
        v = xown[rows, :].astype(F32)
        dv, dg, db = norm_back(v, sum_rows(3, ps_a, i), gains[0:1, :])
        oblk_i[rows, :] = (dr1[rows, :] + dv).astype(BF)
        ngrad[0:1, :] += dg
        ngrad[1:2, :] += db

    n_r = [nr.take() for _ in range(3)]
    targets = (
        [dev(x, y, (z + dz) % 4, (c + dc) % 2) for dz in range(4) for dc in range(2) if dz or dc],
        [dev((x + k) % 4, y, z, c) for k in (1, 2, 3)],
        [dev(x, (y + k) % 4, z, c) for k in (1, 2, 3)],
    )
    places = (0, 7, 10)

    def norm_send(stage):
        for j, to in enumerate(targets[stage]):
            send(ngrad, nrec.at[places[stage] + j], to, n_r[stage], "norm")

    def norm_add(stage):
        flush("norm")
        count = len(targets[stage])
        got(nrec.at[pl.ds(places[stage], count)], n_r[stage])
        v = ngrad[...]
        for j in range(count):
            v = v + nrec[places[stage] + j]
        ngrad[...] = v

    out_start(1, oblk_i, ig_h)
    norm_send(0)
    out_three(0, bo_h)
    scatter_two(S_DOWN)
    out_two(1, ig_h)
    norm_add(0)
    norm_send(1)
    scatter_two(S_UP)
    out_three(1, ig_h)
    norm_add(1)
    norm_send(2)
    scatter_two(S_OUT)
    scatter_two(S_QKV)
    norm_add(2)
    gn_o[...] = ngrad[:, ds(d_at * 128, 128)]

    def put(src, dst):
        cp = pltpu.make_async_copy(src, dst, lsem.at[nl.take()])
        cp.start()
        return cp

    scatter_end(S_DOWN)
    puts = [put(wf_d, gd_h)]
    scatter_end(S_UP)
    puts.append(put(wf_u, gu_h))
    scatter_end(S_QKV)
    puts.append(put(wf_q, gq_h))
    scatter_end(S_OUT)
    puts.append(put(wf_o, go_h))
    out_end(0, bo_h)
    out_end(1, ig_h)
    for cp in puts:
        cp.wait()
    flush()
    assert nr.n <= N_RECV and nl.n <= N_LOCAL


def run_layer(tokens, cotangent, group_sizes, prefix_lens, solution_lens, norms, w_qkv, w_out, w_up, w_down):
    hbm = pl.BlockSpec(memory_space=pltpu.HBM)
    vmem = pl.BlockSpec(memory_space=pltpu.VMEM)
    smem = pl.BlockSpec(memory_space=pltpu.SMEM)
    buf = lambda s, t=BF: pltpu.VMEM(s, t)
    width = lambda p: (p[2], SHARD[p[0]][1])
    scratch = [buf((3, 128, 256), F32), buf((256, 128), F32), buf((128, 1024), F32), buf((1024, 128), F32)]
    scratch += [buf(s) for s in SHARD]
    scratch += [buf((4, 2, 2) + s) for s in SHARD]
    scratch += [buf(((4, 4) if p[3] else (3, 2, 2)) + width(p)) for p in SCATTER]
    scratch += [buf((4,) + width(p)) for p in SCATTER]
    scratch += [
        buf((ROWS, D)), buf((ROWS, D)), buf((ROWS, ROWS)), buf((ROWS, D)), buf((3, ROWS, 256)),
        buf((ROWS, 256)), buf((2, ROWS, ROWS), F32), buf((ROWS, D)), buf((ROWS, 1024)), buf((ROWS, 1024)),
        buf((ROWS, 1024), F32), buf((ROWS, D)), buf((ROWS, D)), buf((4, 2, 2, 1024, 128)),
    ]
    scratch += [buf((4, 256, 512))] * 3
    scratch += [buf((2 if F_SUM else 3, 64, D))] * 3
    scratch += [buf((4, 2, 32, 512))] * 3
    scratch += [
        buf((64, D)), buf((64, D), F32), buf((64, D), F32), buf((ROWS, 256)), buf((ROWS, 768)),
        buf((ROWS, ROWS)), buf((8, 128), F32), buf((16, 8, 128), F32), buf((8, D), F32),
        buf((8, D), F32), buf((13, 8, D), F32), buf((64, D)), buf((64, D)),
    ]
    scratch += [pltpu.SemaphoreType.DMA((n,)) for n in (N_SEND, N_RECV, N_LOCAL)]
    out_shape = [
        jax.ShapeDtypeStruct((ROWS, D), BF), jax.ShapeDtypeStruct((ROWS, D), BF),
        jax.ShapeDtypeStruct((3, 128, 256), F32), jax.ShapeDtypeStruct((256, 128), F32),
        jax.ShapeDtypeStruct((128, 1024), F32), jax.ShapeDtypeStruct((1024, 128), F32),
        jax.ShapeDtypeStruct((8, 128), F32),
    ]
    return pl.pallas_call(
        kernel,
        out_shape=out_shape,
        in_specs=[hbm, hbm, smem, smem, smem, vmem, hbm, hbm, hbm, hbm],
        out_specs=[hbm] * 6 + [vmem],
        scratch_shapes=scratch,
        compiler_params=pltpu.CompilerParams(
            collective_id=0, has_side_effects=True, vmem_limit_bytes=63 * 2**20),
    )(tokens, cotangent, group_sizes, prefix_lens, solution_lens, norms, w_qkv, w_out, w_up, w_down)


def adamw(weight, grad_in, first_old, second_old, step_rate, weight_decay):
    first_new = BETA_ONE * first_old + (1.0 - BETA_ONE) * grad_in
    second_new = BETA_TWO * second_old + (1.0 - BETA_TWO) * grad_in * grad_in
    corr_one = 1.0 - BETA_ONE**STEP
    corr_two = 1.0 - BETA_TWO**STEP
    step_dir = first_new / corr_one / (jnp.sqrt(second_new / corr_two) + ADAM_EPS)
    weight_new = weight - step_rate * (step_dir + weight_decay * weight)
    return (grad_in, first_new, second_new, weight_new, weight_new.astype(jnp.bfloat16))


RATES = ((RATE_QKV, DECAY_RATE), (RATE_OUT, DECAY_RATE), (RATE_UP, DECAY_RATE), (RATE_DOWN, DECAY_RATE),
         (RATE_NORMS, 0.0))


def finish_kernel(bo, ig, *refs):
    ins, outs = refs[:20], refs[20:]
    outs[0][...] = bo[...]
    outs[1][...] = ig[...].astype(F32)
    for k, (rate, decay) in enumerate(RATES):
        w, g, m, v = (r[...] for r in ins[4 * k:4 * k + 4])
        if k == 4:
            g = g[0:4, :]
        for o, r in zip(outs[2 + 5 * k:7 + 5 * k], adamw(w, g, m, v, rate, decay)):
            o[...] = r


def finish(block_out, input_grad, sets):
    steps = 2
    whole = lambda s: pl.BlockSpec(s, lambda i: (0, 0))
    blocks = [
        pl.BlockSpec((3, 128 // steps, 256), lambda i: (0, i, 0)),
        pl.BlockSpec((256 // steps, 128), lambda i: (i, 0)),
        pl.BlockSpec((128 // steps, 1024), lambda i: (i, 0)),
        pl.BlockSpec((1024 // steps, 128), lambda i: (i, 0)),
        whole((4, 128)),
    ]
    rows = pl.BlockSpec((ROWS // steps, D), lambda i: (i, 0))
    in_specs, out_specs = [rows, rows], [rows, rows]
    out_shape = [jax.ShapeDtypeStruct((ROWS, D), BF), jax.ShapeDtypeStruct((ROWS, D), F32)]
    args = [block_out, input_grad]
    for spec, (w, g, m, v) in zip(blocks, sets):
        args += [w, g, m, v]
        in_specs += [spec, whole((8, 128)) if g.shape == (8, 128) else spec, spec, spec]
        out_specs += [spec] * 5
        out_shape += [jax.ShapeDtypeStruct(w.shape, F32)] * 4 + [jax.ShapeDtypeStruct(w.shape, BF)]
    return pl.pallas_call(
        finish_kernel, grid=(steps,), out_shape=out_shape, in_specs=in_specs, out_specs=out_specs,
        compiler_params=pltpu.CompilerParams(vmem_limit_bytes=63 * 2**20),
    )(*args)


def per_device(
    tokens, cotangent, group_sizes, prefix_lens, solution_lens,
    w_qkv, w_out, w_up, w_down, norms,
    first_qkv, second_qkv, first_out, second_out,
    first_up, second_up, first_down, second_down, first_norms, second_norms,
):
    block_out, input_grad, grad_qkv, grad_out, grad_up, grad_down, grad_norms = run_layer(
        tokens, cotangent, group_sizes, prefix_lens, solution_lens, norms, w_qkv, w_out, w_up, w_down)
    sets = (
        (w_qkv, grad_qkv, first_qkv, second_qkv),
        (w_out, grad_out, first_out, second_out),
        (w_up, grad_up, first_up, second_up),
        (w_down, grad_down, first_down, second_down),
        (norms, grad_norms, first_norms, second_norms),
    )
    return tuple(finish(block_out, input_grad, sets))


def solution(mesh):
    row, mat = P("dp", None), P("tensor", "dp")
    qkv, up, nrm = P(None, "dp", "tensor"), P("dp", "tensor"), P(None, "dp")
    return jax.shard_map(
        per_device,
        mesh=mesh,
        in_specs=(row, row, P("dp"), P("dp"), row, qkv, mat, up, mat, nrm,
                  qkv, qkv, mat, mat, up, up, mat, mat, nrm, nrm),
        out_specs=(row, row) + (qkv,) * 5 + (mat,) * 5 + (up,) * 5 + (mat,) * 5 + (nrm,) * 5,
        check_vma=False,
    )
```

```python
import functools

import jax
import jax.numpy as jnp
from jax import lax
from jax.experimental import pallas as pl
from jax.experimental.pallas import tpu as pltpu
from jax.sharding import PartitionSpec as P

HD = 128
STEP = 5
ROWS = 512
D = 2048
NEG_FILL = -1e30
BETA_ONE = 0.5
BETA_TWO = 0.5
ADAM_EPS = 1e-08
NORM_EPS = 1e-05
DECAY_RATE = 0.1
RATE_QKV = 0.02
RATE_OUT = 0.15
RATE_UP = 0.02
RATE_DOWN = 0.01
RATE_NORMS = 0.3
SCALE = HD ** (-0.5)
GELU_K = 0.7978845608028654
GELU_C = 0.044715

BF = jnp.bfloat16
F32 = jnp.float32
MESH = pl.DeviceIdType.MESH
NT = (((1,), (1,)), ((), ()))
TN = (((0,), (0,)), ((), ()))
NN = (((1,), (0,)), ((), ()))

SHARD = ((128, 256), (128, 256), (128, 256), (256, 128), (128, 1024), (1024, 128))
Q_, K_, V_, O_, U_, D_ = range(6)
G_QK = ((Q_, 0, 64, True), (Q_, 64, 64, False), (K_, 0, 64, True), (K_, 64, 64, False))
G_V = ((V_, 0, 64, True), (V_, 64, 64, False))
G_OUT = ((O_, 0, 128, True), (O_, 128, 128, False))
G_UP = ((U_, 0, 64, True), (U_, 64, 64, False))
G_DOWN = ((D_, 0, 512, True), (D_, 512, 512, False))
GATHER = G_QK + G_V + G_OUT + G_UP + G_DOWN
S_DOWN = ((D_, 0, 512, True), (D_, 512, 512, False))
S_UP = ((U_, 0, 64, True), (U_, 64, 64, False))
S_QKV = ((Q_, 0, 128, True), (K_, 0, 128, False), (V_, 0, 64, True), (V_, 64, 64, False))
S_OUT = ((O_, 0, 128, True), (O_, 128, 128, False))
SCATTER = S_DOWN + S_UP + S_QKV + S_OUT


def dot(a, b, dims=NN):
    return lax.dot_general(a, b, dims, preferred_element_type=F32)


def ds(start, size, mult=None):
    if not isinstance(start, int):
        start = pl.multiple_of(start, mult or size)
    return pl.ds(start, size)


F_SUM, F_SPREAD, F_OUT = 0, 1, 1
N_SEND = 200
N_RECV = 180
N_LOCAL = 16


class Counter:
    def __init__(self):
        self.n = 0

    def take(self, k=1):
        base = self.n
        self.n += k
        return base


def kernel(*refs):
    it = iter(refs)
    take = lambda n: [next(it) for _ in range(n)]
    tok_h, cot_h, size_s, prefix_s, lens_s, nrm_in = take(6)
    wq_h, wo_h, wu_h, wd_h = take(4)
    bo_h, ig_h, gq_h, go_h, gu_h, gd_h, gn_o = take(7)
    wf_q, wf_o, wf_u, wf_d = take(4)
    own = take(6)
    gat = take(6)
    rcv1 = dict(zip(SCATTER, take(len(SCATTER))))
    rcv2 = dict(zip(SCATTER, take(len(SCATTER))))
    tok, back, bias, a1, qkv, mixed, probs, a2, hid, dup, slope, ps_a, ps_b, gdb = take(14)
    rc = take(3)
    rz = take(3)
    relay = take(3)
    xown, r1, dr1, ybuf, dqkv, ds_s, nst, nbuf, gains, ngrad, nrec, oblk_b, oblk_i = take(13)
    ssem, rsem, lsem = take(3)
    rc = (rc[0], rc[1], rc[2], rc[0])
    rz = (rz[0], rz[1], rz[2], rz[0])
    relay = (relay[0], relay[1], relay[2], relay[0])
    dt, pb_s = tok, bias
    grad = {D_: gdb, **{k: gat[k] for k in (Q_, K_, V_, O_, U_)}}

    d_at = lax.axis_index("dp")
    t_at = lax.axis_index("tensor")
    x = d_at // 4
    yl = (d_at // 2) % 2
    c = d_at % 2
    z = t_at // 2
    yh = t_at % 2
    y = yh * 2 + yl
    other = 1 - c

    def dev(px, py, pz, pc):
        return {"dp": (px * 2 + py % 2) * 2 + pc, "tensor": pz * 2 + py // 2}

    nr, nl = Counter(), Counter()
    pending, free = [], list(range(N_SEND))[::-1]

    def rcopy(src, dst, to, si, ri):
        return pltpu.make_async_remote_copy(
            src_ref=src, dst_ref=dst, send_sem=ssem.at[si], recv_sem=rsem.at[ri],
            device_id=to, device_id_type=MESH)

    def send(src, dst, to, ri, tag=""):
        si = free.pop()
        cp = rcopy(src, dst, to, si, ri)
        cp.start()
        pending.append((tag, cp, None, si))

    def send_or_local(here, src, dst, to, ri, tag=""):
        si = free.pop()
        cp = rcopy(src, dst, to, si, ri)
        away = jnp.logical_not(here)

        @pl.when(here)
        def _():
            pltpu.make_async_copy(src, dst, rsem.at[ri]).start()

        @pl.when(away)
        def _():
            cp.start()

        pending.append((tag, cp, away, si))

    def send_if(cond, src, dst, to, ri, tag=""):
        si = free.pop()
        cp = rcopy(src, dst, to, si, ri)

        @pl.when(cond)
        def _():
            cp.start()

        pending.append((tag, cp, cond, si))

    def flush(tag=None):
        for item in pending[:]:
            kind, cp, cond, si = item
            if tag is None or kind == tag:
                pending.remove(item)
                free.append(si)
                if cond is None:
                    cp.wait_send()
                else:
                    pl.when(cond)(cp.wait_send)

    def got(dst, ri):
        rcopy(dst, dst, dev(x, y, z, other), 0, ri).wait_recv()

    def load(src, dst):
        cp = pltpu.make_async_copy(src, dst, lsem.at[nl.take()])
        cp.start()
        return cp

    home = c == yh
    my_row = c * 256 + z * 64
    ld_q = load(wq_h, wf_q)
    ld_o = load(wo_h, wf_o)
    ld_t = pltpu.make_async_copy(tok_h, tok, lsem.at[nl.take()])
    ld_c = pltpu.make_async_copy(cot_h, back, lsem.at[nl.take()])
    pl.when(home)(ld_t.start)
    ld_u = load(wu_h, wf_u)
    ld_d = load(wd_h, wf_d)
    pl.when(home)(ld_c.start)

    yp = yh * 2 + (1 - yl)
    peers = [dev(x, y, z, other)]
    for k in (1, 2, 3):
        for cc in (0, 1):
            peers.append(dev((x + k) % 4, y, z, cc))
            peers.append(dev(x, (y + k) % 4, z, cc))
            peers.append(dev(x, y, (z + k) % 4, cc))
            peers.append(dev((x + k) % 4, yp, z, cc))
    barrier = pltpu.get_barrier_semaphore()
    for peer in peers:
        pl.semaphore_signal(barrier, inc=1, device_id=peer, device_id_type=MESH)
    nst[0:4, :] = nrm_in[...].astype(BF).astype(F32)
    nst[4:8, :] = jnp.zeros((4, 128), F32)
    ld_q.wait()
    for j in range(3):
        own[j][...] = wf_q[j].astype(BF)
    ld_o.wait()
    own[O_][...] = wf_o[...].astype(BF)
    pl.when(home)(ld_t.wait)
    pl.semaphore_wait(barrier, len(peers))

    g1_r = {p: nr.take() for p in GATHER}
    g2_r = {p: nr.take(3) for p in GATHER}

    def gather_one(parts):
        for p in parts:
            k, r0, rn, x_first = p
            rows = pl.ds(r0, rn)
            for j in range(4):
                if x_first:
                    to = dev((x + j) % 4, y, z, yh)
                else:
                    to = dev(x, (y + j) % 4, z, yh)
                src, dst = own[k].at[rows], gat[k].at[x, yl, c, rows]
                if j == 0:
                    send_or_local(home, src, dst, to, g1_r[p], "gather")
                else:
                    send(src, dst, to, g1_r[p], "gather")

    r_at = (y + 4 - 2 * c) % 4

    def gather_two(parts):
        for p in parts:
            k, r0, rn, x_first = p
            rows = pl.ds(r0, rn)
            if x_first:
                part = gat[k].at[:, yl, :, rows]

                @pl.when(home)
                def _():
                    got(part, g1_r[p])

                for step in (1, 3):
                    send_if(home, part, part, dev(x, (y + step) % 4, z, c), g2_r[p], "gather")
            else:
                part = gat[k].at[x, :, :, rows]
                got(part, g1_r[p])
                send(part, part, dev((x + 1) % 4, y, z, c), g2_r[p], "gather")
                send(part, part, dev((x + 3) % 4, y, z, c), g2_r[p] + 1, "gather")

    def gather_three(parts):
        for p in parts:
            k, r0, rn, x_first = p
            rows = pl.ds(r0, rn)
            if x_first:
                src_l = 1 - r_at % 2
                got(gat[k].at[:, src_l, :, rows], g2_r[p])
                half = jnp.where((r_at == 0) | (r_at == 3), 1, 0)
                part = gat[k].at[pl.ds(2 * half, 2), src_l, :, rows]
                to = dev(x, (2 * c + 3 - r_at % 2) % 4, z, c)
                send(part, part, to, g2_r[p] + 1, "gather")
            else:
                xm, xp = (x + 3) % 4, (x + 1) % 4
                got(gat[k].at[xm, :, :, rows], g2_r[p])
                part = gat[k].at[xm, 0, :, rows]
                send(part, part, dev(xp, y, z, c), g2_r[p] + 2, "gather")
                got(gat[k].at[xp, :, :, rows], g2_r[p] + 1)
                part = gat[k].at[xp, 1, :, rows]
                send(part, part, dev(xm, y, z, c), g2_r[p] + 2, "gather")

    def gather_end(parts):
        for p in parts:
            k, r0, rn, x_first = p
            rows = pl.ds(r0, rn)
            if x_first:
                @pl.when(r_at >= 2)
                def _():
                    got(gat[k].at[:, r_at % 2, :, rows], g2_r[p] + 1)
            else:
                got(gat[k].at[(x + 2) % 4, :, :, rows], g2_r[p] + 2)

    gather_one(G_QK)
    gather_one(G_V)

    tok_r = nr.take(3)

    def share(i, buf):
        send_if(home, buf, buf, dev(x, y, z, other), tok_r + i, "group")

    def shared(i, buf):
        @pl.when(jnp.logical_not(home))
        def _():
            got(buf, tok_r + i)

    norm_r = nr.take()
    pltpu.make_async_copy(nst, nbuf.at[d_at], rsem.at[norm_r]).start()
    for dx in range(4):
        for dl in (0, 1):
            for dc in (0, 1):
                if dx or dl or dc:
                    to = dev((x + dx) % 4, yh * 2 + (yl + dl) % 2, z, (c + dc) % 2)
                    send(nst, nbuf.at[d_at], to, norm_r)
    share(0, tok)
    gather_one(G_OUT)

    ld_u.wait()

    @pl.loop(0, 8)
    def _(i):
        own[U_][ds(i * 16, 16), :] = wf_u[ds(i * 16, 16), :].astype(BF)

    @pl.when(home)
    def _():
        ends = []
        total = prefix_s[0]
        for i in range(16):
            total = total + jnp.where(i < size_s[0], lens_s[0, i], 0)
            ends.append(total)

        def segment(pos):
            seg = jnp.where(pos >= ends[0], 1, 0)
            for i in range(1, 16):
                seg = seg + jnp.where(pos >= ends[i], 1, 0)
            return jnp.where(pos < prefix_s[0], -1, seg)

        row_pos = lax.broadcasted_iota(jnp.int32, (8, ROWS), 1)
        row_seg = segment(row_pos)[0:1, :]
        row_pos = row_pos[0:1, :]

        @pl.loop(0, 8)
        def _(i):
            rows = ds(i * 64, 64)
            pos = lax.broadcasted_iota(jnp.int32, (64, 128), 0) + i * 64
            seg = jnp.concatenate([segment(pos)] * 4, axis=1)
            at = jnp.concatenate([pos] * 4, axis=1)
            linked = (seg == row_seg) | (row_seg < 0)
            live = (at < total) & (row_pos < total) & (row_pos <= at)
            allowed = (linked & live) | (row_pos == at)
            bias[rows, :] = jnp.where(allowed, 0.0, NEG_FILL).astype(BF)

        ld_c.wait()

        @pl.loop(0, 16)
        def _(i):
            rows = ds(i * 32, 32)
            pos = lax.broadcasted_iota(jnp.int32, (32, 128), 0) + i * 32
            keep = jnp.where(pos < total, 1.0, 0.0)
            keep = jnp.concatenate([keep] * 16, axis=1)
            back[rows, :] = (back[rows, :].astype(F32) * keep).astype(BF)

    share(1, bias)
    share(2, back)

    got(nbuf, norm_r)
    for i in range(16):
        gains[:, i * 128:(i + 1) * 128] = nbuf[i]

    gather_two(G_QK)
    gather_two(G_V)

    shared(0, tok)

    @pl.loop(0, ROWS // 32)
    def _(i):
        rows = ds(i * 32, 32)
        v = tok[rows, :].astype(F32)
        cen = v - jnp.mean(v, axis=-1, keepdims=True)
        var = jnp.mean(cen * cen, axis=-1, keepdims=True)
        a1[rows, :] = (cen * lax.rsqrt(var + NORM_EPS) * gains[0:1, :] + gains[1:2, :]).astype(BF)

    for i in range(4):
        xown[i * 16:(i + 1) * 16, :] = tok[ds(my_row + i * 16, 16), :]

    ld_d.wait()

    @pl.loop(0, 8)
    def _(i):
        own[D_][ds(i * 128, 128), :] = wf_d[ds(i * 128, 128), :].astype(BF)

    gather_three(G_QK)
    gather_three(G_V)
    gather_two(G_OUT)
    gather_one(G_UP)

    def project(j):
        v = dot(a1[...], gat[j][...].reshape(D, 256))
        if j == Q_:
            v = v * SCALE
        qkv[j] = v.astype(BF)

    gather_end(G_QK)
    gather_end(G_V)
    project(Q_)
    project(K_)
    project(V_)
    gather_three(G_OUT)
    gather_two(G_UP)
    gather_one(G_DOWN)
    shared(1, bias)

    for h in range(2):
        cols = slice(h * HD, (h + 1) * HD)

        @pl.loop(0, 4)
        def _(i):
            rows = ds(i * 128, 128)
            s = dot(qkv[0, rows, cols], qkv[1, :, cols], NT) + bias[rows, :].astype(F32)
            w = jnp.exp(s - jnp.max(s, axis=-1, keepdims=True))
            probs[h, rows, :] = w / jnp.sum(w, axis=-1, keepdims=True)

    for h in range(2):
        cols = slice(h * HD, (h + 1) * HD)
        mixed[:, cols] = dot(probs[h].astype(BF), qkv[2, :, cols]).astype(BF)

    rc_r = [nr.take(4) for _ in range(4)]
    rz_r = [nr.take() for _ in range(4)]
    rl_r = [nr.take(4) for _ in range(4)]

    def z_block(dz):
        return c * 256 + (z + dz) % 4 * 64

    def sum_combine(k, ps, j):
        cols = pl.ds(j * 512, 512)
        got(rc[k].at[j], rc_r[k] + j)
        for dz in (2, 1, 3, 0):
            rows = ds(z_block(dz), 64)
            from_other = rc[k][j, ds((z + dz) % 4 * 64, 64), :].astype(F32)
            ps[rows, cols] = (ps[rows, cols].astype(F32) + from_other).astype(BF)

    def sum_relay(k, ps, j):
        cols = pl.ds(j * 512, 512)
        if not F_SUM:
            for dz in (2, 1, 3):
                send(ps.at[ds(z_block(dz), 64), cols], rz[k].at[dz - 1, :, cols], dev(x, y, (z + dz) % 4, c),
                     rz_r[k], f"sum{k}")
            return
        for half, step in ((0, 1), (1, 3)):
            send(ps.at[ds(z_block(2) + half * 32, 32), cols], relay[k].at[j, half],
                 dev(x, y, (z + step) % 4, c), rl_r[k] + j, f"sum{k}")

    def sum_pass(k, ps, j):
        if not F_SUM:
            return
        cols = pl.ds(j * 512, 512)
        got(relay[k].at[j], rl_r[k] + j)
        for half, step in ((0, 1), (1, 3)):
            rows = ds(z_block(step) + half * 32, 32)
            ps[rows, cols] = (ps[rows, cols].astype(F32) + relay[k][j, half].astype(F32)).astype(BF)
            send(ps.at[ds(z_block(step), 64), cols], rz[k].at[half, :, cols],
                 dev(x, y, (z + step) % 4, c), rz_r[k], f"sum{k}")

    def sum_part(k, ps, compute, j):
        cols = pl.ds(j * 512, 512)
        ps[:, cols] = compute(j).astype(BF)
        half = ps.at[ds(other * 256, 256), cols]
        send(half, rc[k].at[j], dev(x, y, z, other), rc_r[k] + j, f"sum{k}")

    def sum_run(k, ps, compute):
        for j in range(7):
            if j < 4:
                sum_part(k, ps, compute, j)
            if 1 <= j < 5:
                sum_combine(k, ps, j - 1)
                sum_relay(k, ps, j - 1)
            if 2 <= j < 6:
                sum_pass(k, ps, j - 2)

    def sum_wait(k):
        got(rz[k], rz_r[k])

    def sum_rows(k, ps, i):
        rows = ds(i * 16, 16)
        v = ps[ds(my_row + i * 16, 16), :].astype(F32)
        for j in range(2 if F_SUM else 3):
            v = v + rz[k][j, rows, :].astype(F32)
        return v

    ag_r = [nr.take(3) for _ in range(2)]
    ac_r = [nr.take() for _ in range(2)]

    def spread_start(k, buf):
        part = buf.at[ds(my_row, 64), :]
        for half, step in ((0, 1), (1, 3)):
            send(part, part, dev(x, y, (z + step) % 4, c), ag_r[k] + half)
        if not F_SPREAD:
            send(part, part, dev(x, y, (z + 2) % 4, c), ag_r[k] + 2)
        send(part, part, dev(x, y, z, other), ac_r[k])

    def spread_pass(k, buf):
        base = c * 256
        for half, step in ((0, 1), (1, 3)):
            at = base + (z + 4 - step) % 4 * 64
            part = buf.at[ds(at, 64), :]
            got(part, ag_r[k] + half)
            piece = buf.at[ds(at + half * 32, 32), :]
            if F_SPREAD:
                send(piece, piece, dev(x, y, (z + step) % 4, c), ag_r[k] + 2)
            send(part, part, dev(x, y, z, other), ac_r[k])
        part = buf.at[ds(base + (z + 2) % 4 * 64, 64), :]
        got(part, ag_r[k] + 2)
        send(part, part, dev(x, y, z, other), ac_r[k])

    def spread_end(k, buf):
        got(buf.at[ds(other * 256, 256), :], ac_r[k])

    def attn_out(j):
        w = jnp.concatenate([gat[O_][j, a, b] for a in range(2) for b in range(2)], axis=1)
        return dot(mixed[...], w)

    gather_end(G_OUT)
    flush("group")
    sum_run(0, ps_a, attn_out)
    gather_three(G_UP)
    gather_two(G_DOWN)
    sum_wait(0)

    @pl.loop(0, 4)
    def _(i):
        rows = ds(i * 16, 16)
        v = xown[rows, :].astype(F32) + sum_rows(0, ps_a, i)
        r1[rows, :] = v
        cen = v - jnp.mean(v, axis=-1, keepdims=True)
        var = jnp.mean(cen * cen, axis=-1, keepdims=True)
        n = cen * lax.rsqrt(var + NORM_EPS) * gains[2:3, :] + gains[3:4, :]
        a2[ds(my_row + i * 16, 16), :] = n.astype(BF)

    spread_start(0, a2)
    spread_pass(0, a2)
    gather_three(G_DOWN)

    gather_end(G_UP)
    spread_end(0, a2)

    @pl.loop(0, 4)
    def _(i):
        cols = ds(i * 256, 256)
        u = dot(a2[...], gat[U_][:, :, :, :, cols].reshape(D, 256))
        th = jnp.tanh(GELU_K * (u + GELU_C * u * u * u))
        hid[:, cols] = (0.5 * u * (1.0 + th)).astype(BF)
        slope[:, cols] = 0.5 * (1.0 + th) + 0.5 * u * (1.0 - th * th) * (GELU_K * (1.0 + 3.0 * GELU_C * u * u))

    shared(2, back)

    s1_r = {p: nr.take() for p in SCATTER}
    s2_r = {p: nr.take() for p in SCATTER}

    def scatter_one(parts):
        for p in parts:
            k, r0, rn, y_first = p
            rows = pl.ds(r0, rn)
            if y_first:
                for tl in range(2):
                    for tc in range(2):
                        here = home & (yl == tl) & (c == tc)
                        src, dst = grad[k].at[:, tl, tc, rows], rcv1[p].at[y]
                        send_or_local(here, src, dst, dev(x, 2 * c + tl, z, tc), s1_r[p])
            else:
                for dx in (2, 1, 3):
                    px = (x + dx) % 4
                    send(grad[k].at[px, :, :, rows], rcv1[p].at[dx - 1], dev(px, y, z, c), s1_r[p])

    def add_up(parts, out, shape):
        step = 16384 // shape[1]

        @pl.loop(0, shape[0] // step)
        def _(i):
            rows = ds(i * step, step)
            v = parts[0][rows, :].astype(F32)
            for q in parts[1:]:
                v = v + q[rows, :].astype(F32)
            out[rows, :] = v.astype(out.dtype)

    def scatter_two(parts):
        for p in parts:
            scatter_two_of(p)

    def scatter_two_of(p):
        k, r0, rn, y_first = p
        shape = (rn, SHARD[k][1])
        if y_first:
            got(rcv1[p], s1_r[p])
            for dx in (2, 1, 3, 0):
                px = (x + dx) % 4
                out = rcv1[p].at[0, px]
                add_up([rcv1[p].at[sy, px] for sy in range(4)], out, shape)
                if dx == 0:
                    pltpu.make_async_copy(out, rcv2[p].at[x], rsem.at[s2_r[p]]).start()
                else:
                    send(out, rcv2[p].at[x], dev(px, y, z, c), s2_r[p])
        else:
            got(rcv1[p], s1_r[p])
            for a in range(2):
                for b in range(2):
                    out = rcv1[p].at[0, a, b]
                    mine = grad[k].at[x, a, b, pl.ds(r0, rn)]
                    add_up([mine] + [rcv1[p].at[j, a, b] for j in range(3)], out, shape)
                    here = home & (yl == a) & (c == b)
                    send_or_local(here, out, rcv2[p].at[y], dev(x, 2 * c + a, z, b), s2_r[p])

    stage = {Q_: wf_q.at[0], K_: wf_q.at[1], V_: wf_q.at[2], O_: wf_o, U_: wf_u, D_: wf_d}

    def scatter_end(parts):
        for p in parts:
            k, r0, rn, _ = p
            got(rcv2[p], s2_r[p])
            add_up([rcv2[p].at[j] for j in range(4)], stage[k].at[pl.ds(r0, rn)], (rn, SHARD[k][1]))

    @pl.loop(0, 4)
    def _(i):
        v = dot(hid[...], back[:, ds(i * 512, 512)], TN).astype(BF)
        for n in range(4):
            gdb[i, n // 2, n % 2] = v[:, n * 128:(n + 1) * 128]

    gather_end(G_DOWN)
    scatter_one(S_DOWN)

    @pl.loop(0, 4)
    def _(i):
        cols = ds(i * 256, 256)
        w = jnp.concatenate([gat[D_][a, b, e, cols, :] for a in range(4) for b in range(2) for e in range(2)], axis=1)
        dup[:, cols] = (dot(back[...], w, NT) * slope[:, cols]).astype(BF)

    def entry(j):
        return dot(dup[...], gat[U_][j].reshape(512, 1024), NT)

    def down(j):
        w = jnp.concatenate([gat[D_][j, a, b] for a in range(2) for b in range(2)], axis=1)
        return dot(hid[...], w)

    flush("sum0")
    sum_run(1, ps_a, entry)
    flush("gather")

    @pl.loop(0, 4)
    def _(i):
        v = dot(a2[:, ds(i * 512, 512)], dup[...], TN).astype(BF)
        for n in range(4):
            gat[U_][i, n // 2, n % 2] = v[n * 128:(n + 1) * 128]

    scatter_one(S_UP)

    def norm_back(v, dy, gain):
        cen = v - jnp.mean(v, axis=-1, keepdims=True)
        rs = lax.rsqrt(jnp.mean(cen * cen, axis=-1, keepdims=True) + NORM_EPS)
        xh = cen * rs
        e = dy * gain
        dv = rs * (e - jnp.mean(e, axis=-1, keepdims=True) - xh * jnp.mean(e * xh, axis=-1, keepdims=True))
        return dv, jnp.sum(dy * xh, axis=0, keepdims=True), jnp.sum(dy, axis=0, keepdims=True)

    ngrad[...] = jnp.zeros_like(ngrad)
    sum_wait(1)

    @pl.loop(0, 4)
    def _(i):
        rows = ds(i * 16, 16)
        mine = ds(my_row + i * 16, 16)
        dv, dg, db = norm_back(r1[rows, :], sum_rows(1, ps_a, i), gains[2:3, :])
        v = back[mine, :].astype(F32) + dv
        dr1[rows, :] = v
        dt[mine, :] = v.astype(BF)
        ngrad[2:3, :] += dg
        ngrad[3:4, :] += db

    spread_start(1, dt)

    o1_r = [nr.take(8) for _ in range(2)]

    def out_rows(out, sz, sc, first=0, rows=64):
        return out.at[ds(sc * 256 + sz % 4 * 64 + first, rows), :]

    def out_start(k, blk, out):
        part = out.at[ds(my_row, 64), :]
        send(blk, part, dev(x, (y + 2) % 4, z, yh), o1_r[k] + c)
        for half, step in ((0, 1), (1, 3)):
            send(blk, part, dev(x, y, (z + step) % 4, yh), o1_r[k] + 2 + half * 2 + c)
        if not F_OUT:
            send(blk, part, dev(x, y, (z + 2) % 4, yh), o1_r[k] + 6 + c)
        send_or_local(home, blk, part, dev(x, y, z, yh), o1_r[k] + c)

    def out_two(k, out):
        for sc in range(2):
            part = out_rows(out, z, sc)
            got(part, o1_r[k] + sc)
            for half, step in ((0, 1), (1, 3)):
                send_if(jnp.logical_not(home), part, part, dev(x, y, (z + step) % 4, c),
                        o1_r[k] + 2 + half * 2 + sc)
            if not F_OUT:
                send_if(jnp.logical_not(home), part, part, dev(x, y, (z + 2) % 4, c), o1_r[k] + 6 + sc)

    def out_three(k, out):
        for sc in range(2):
            for half, step in ((0, 1), (1, 3)):
                got(out_rows(out, z + 4 - step, sc), o1_r[k] + 2 + half * 2 + sc)
                if not F_OUT:
                    continue
                piece = out_rows(out, z + 4 - step, sc, half * 32, 32)
                send(piece, piece, dev(x, y, (z + step) % 4, c), o1_r[k] + 6 + sc)

    def out_end(k, out):
        for sc in range(2):
            got(out_rows(out, z + 2, sc), o1_r[k] + 6 + sc)

    for j in range(4):
        sum_part(2, ps_b, down, j)
    spread_pass(1, dt)
    for j in range(4):
        sum_combine(2, ps_b, j)
        sum_relay(2, ps_b, j)
    spread_end(1, dt)

    @pl.loop(0, 2)
    def _(i):
        rows = ds(i * 256, 256)
        w = jnp.concatenate([gat[O_][a, b, e] for a in range(4) for b in range(2) for e in range(2)], axis=1)
        ybuf[rows, :] = dot(dt[rows, :], w, NT).astype(BF)

    for h in range(2):
        cols = slice(h * HD, (h + 1) * HD)

        @pl.loop(0, 4)
        def _(i):
            rows = ds(i * 128, 128)
            p = probs[h, rows, :]
            pb_s[rows, :] = p.astype(BF)
            dp = dot(ybuf[rows, cols], qkv[2, :, cols], NT)
            d_s = (p * (dp - jnp.sum(p * dp, axis=-1, keepdims=True))).astype(BF)
            ds_s[rows, :] = d_s
            dqkv[rows, cols] = dot(d_s, qkv[1, :, cols]).astype(BF)

        dqkv[:, 256 + h * HD:256 + (h + 1) * HD] = dot(ds_s[...], qkv[0, :, cols], TN).astype(BF)
        dqkv[:, 512 + h * HD:512 + (h + 1) * HD] = dot(pb_s[...], ybuf[:, cols], TN).astype(BF)

    def into_norm(j):
        ws = [gat[k][j].reshape(512, 256) for k in range(3)]
        v = dot(dqkv[:, 0:256], ws[0], NT) * SCALE
        v = v + dot(dqkv[:, 256:512], ws[1], NT)
        return v + dot(dqkv[:, 512:768], ws[2], NT)

    flush("sum1")
    for j in range(4):
        sum_pass(2, ps_b, j)
    sum_run(3, ps_a, into_norm)
    sum_wait(2)

    @pl.loop(0, 4)
    def _(i):
        rows = ds(i * 16, 16)
        oblk_b[rows, :] = (r1[rows, :] + sum_rows(2, ps_b, i)).astype(BF)

    out_start(0, oblk_b, bo_h)

    @pl.loop(0, 4)
    def _(i):
        v = dot(mixed[...], dt[:, ds(i * 512, 512)], TN).astype(BF)
        for n in range(4):
            gat[O_][i, n // 2, n % 2] = v[:, n * 128:(n + 1) * 128]

    scatter_one(S_OUT)

    @pl.loop(0, 8)
    def _(i):
        v = dot(a1[:, ds(i * 256, 256)], dqkv[...], TN)
        for k in range(3):
            w = v[:, k * 256:(k + 1) * 256]
            w = (w * SCALE if k == 0 else w).astype(BF)
            gat[k][i // 2, i % 2, 0] = w[:128]
            gat[k][i // 2, i % 2, 1] = w[128:]

    scatter_one([p for p in S_QKV if not p[3]])
    out_two(0, bo_h)

    sum_wait(3)

    @pl.loop(0, 4)
    def _(i):
        rows = ds(i * 16, 16)
        v = xown[rows, :].astype(F32)
        dv, dg, db = norm_back(v, sum_rows(3, ps_a, i), gains[0:1, :])
        oblk_i[rows, :] = (dr1[rows, :] + dv).astype(BF)
        ngrad[0:1, :] += dg
        ngrad[1:2, :] += db

    n_r = [nr.take() for _ in range(3)]
    targets = (
        [dev(x, y, (z + dz) % 4, (c + dc) % 2) for dz in range(4) for dc in range(2) if dz or dc],
        [dev((x + k) % 4, y, z, c) for k in (1, 2, 3)],
        [dev(x, (y + k) % 4, z, c) for k in (1, 2, 3)],
    )
    places = (0, 7, 10)

    def norm_send(stage):
        for j, to in enumerate(targets[stage]):
            send(ngrad, nrec.at[places[stage] + j], to, n_r[stage], "norm")

    def norm_add(stage):
        flush("norm")
        count = len(targets[stage])
        got(nrec.at[pl.ds(places[stage], count)], n_r[stage])
        v = ngrad[...]
        for j in range(count):
            v = v + nrec[places[stage] + j]
        ngrad[...] = v

    out_start(1, oblk_i, ig_h)
    scatter_one([p for p in S_QKV if p[3]])
    norm_send(0)
    out_three(0, bo_h)
    scatter_two(S_DOWN)
    norm_add(0)
    norm_send(1)
    out_two(1, ig_h)
    scatter_two(S_UP)
    scatter_two(S_OUT)
    norm_add(1)
    norm_send(2)
    out_three(1, ig_h)
    scatter_two(S_QKV)
    norm_add(2)
    gn_o[...] = ngrad[:, ds(d_at * 128, 128)]

    def put(src, dst):
        cp = pltpu.make_async_copy(src, dst, lsem.at[nl.take()])
        cp.start()
        return cp

    scatter_end(S_DOWN)
    puts = [put(wf_d, gd_h)]
    scatter_end(S_UP)
    puts.append(put(wf_u, gu_h))
    scatter_end(S_QKV)
    puts.append(put(wf_q, gq_h))
    scatter_end(S_OUT)
    puts.append(put(wf_o, go_h))
    out_end(0, bo_h)
    out_end(1, ig_h)
    for cp in puts:
        cp.wait()
    flush()
    assert nr.n <= N_RECV and nl.n <= N_LOCAL


def run_layer(tokens, cotangent, group_sizes, prefix_lens, solution_lens, norms, w_qkv, w_out, w_up, w_down):
    hbm = pl.BlockSpec(memory_space=pltpu.HBM)
    vmem = pl.BlockSpec(memory_space=pltpu.VMEM)
    smem = pl.BlockSpec(memory_space=pltpu.SMEM)
    buf = lambda s, t=BF: pltpu.VMEM(s, t)
    width = lambda p: (p[2], SHARD[p[0]][1])
    scratch = [buf((3, 128, 256), F32), buf((256, 128), F32), buf((128, 1024), F32), buf((1024, 128), F32)]
    scratch += [buf(s) for s in SHARD]
    scratch += [buf((4, 2, 2) + s) for s in SHARD]
    scratch += [buf(((4, 4) if p[3] else (3, 2, 2)) + width(p)) for p in SCATTER]
    scratch += [buf((4,) + width(p)) for p in SCATTER]
    scratch += [
        buf((ROWS, D)), buf((ROWS, D)), buf((ROWS, ROWS)), buf((ROWS, D)), buf((3, ROWS, 256)),
        buf((ROWS, 256)), buf((2, ROWS, ROWS), F32), buf((ROWS, D)), buf((ROWS, 1024)), buf((ROWS, 1024)),
        buf((ROWS, 1024), F32), buf((ROWS, D)), buf((ROWS, D)), buf((4, 2, 2, 1024, 128)),
    ]
    scratch += [buf((4, 256, 512))] * 3
    scratch += [buf((2 if F_SUM else 3, 64, D))] * 3
    scratch += [buf((4, 2, 32, 512))] * 3
    scratch += [
        buf((64, D)), buf((64, D), F32), buf((64, D), F32), buf((ROWS, 256)), buf((ROWS, 768)),
        buf((ROWS, ROWS)), buf((8, 128), F32), buf((16, 8, 128), F32), buf((8, D), F32),
        buf((8, D), F32), buf((13, 8, D), F32), buf((64, D)), buf((64, D)),
    ]
    scratch += [pltpu.SemaphoreType.DMA((n,)) for n in (N_SEND, N_RECV, N_LOCAL)]
    out_shape = [
        jax.ShapeDtypeStruct((ROWS, D), BF), jax.ShapeDtypeStruct((ROWS, D), BF),
        jax.ShapeDtypeStruct((3, 128, 256), F32), jax.ShapeDtypeStruct((256, 128), F32),
        jax.ShapeDtypeStruct((128, 1024), F32), jax.ShapeDtypeStruct((1024, 128), F32),
        jax.ShapeDtypeStruct((8, 128), F32),
    ]
    return pl.pallas_call(
        kernel,
        out_shape=out_shape,
        in_specs=[hbm, hbm, smem, smem, smem, vmem, hbm, hbm, hbm, hbm],
        out_specs=[hbm] * 6 + [vmem],
        scratch_shapes=scratch,
        compiler_params=pltpu.CompilerParams(
            collective_id=0, has_side_effects=True, vmem_limit_bytes=63 * 2**20),
    )(tokens, cotangent, group_sizes, prefix_lens, solution_lens, norms, w_qkv, w_out, w_up, w_down)


def adamw(weight, grad_in, first_old, second_old, step_rate, weight_decay):
    first_new = BETA_ONE * first_old + (1.0 - BETA_ONE) * grad_in
    second_new = BETA_TWO * second_old + (1.0 - BETA_TWO) * grad_in * grad_in
    corr_one = 1.0 - BETA_ONE**STEP
    corr_two = 1.0 - BETA_TWO**STEP
    step_dir = first_new / corr_one / (jnp.sqrt(second_new / corr_two) + ADAM_EPS)
    weight_new = weight - step_rate * (step_dir + weight_decay * weight)
    return (grad_in, first_new, second_new, weight_new, weight_new.astype(jnp.bfloat16))


RATES = ((RATE_QKV, DECAY_RATE), (RATE_OUT, DECAY_RATE), (RATE_UP, DECAY_RATE), (RATE_DOWN, DECAY_RATE),
         (RATE_NORMS, 0.0))


def finish_kernel(bo, ig, *refs):
    ins, outs = refs[:20], refs[20:]
    outs[0][...] = bo[...]
    outs[1][...] = ig[...].astype(F32)
    for k, (rate, decay) in enumerate(RATES):
        w, g, m, v = (r[...] for r in ins[4 * k:4 * k + 4])
        if k == 4:
            g = g[0:4, :]
        for o, r in zip(outs[2 + 5 * k:7 + 5 * k], adamw(w, g, m, v, rate, decay)):
            o[...] = r


def finish(block_out, input_grad, sets):
    steps = 2
    whole = lambda s: pl.BlockSpec(s, lambda i: (0, 0))
    blocks = [
        pl.BlockSpec((3, 128 // steps, 256), lambda i: (0, i, 0)),
        pl.BlockSpec((256 // steps, 128), lambda i: (i, 0)),
        pl.BlockSpec((128 // steps, 1024), lambda i: (i, 0)),
        pl.BlockSpec((1024 // steps, 128), lambda i: (i, 0)),
        whole((4, 128)),
    ]
    rows = pl.BlockSpec((ROWS // steps, D), lambda i: (i, 0))
    in_specs, out_specs = [rows, rows], [rows, rows]
    out_shape = [jax.ShapeDtypeStruct((ROWS, D), BF), jax.ShapeDtypeStruct((ROWS, D), F32)]
    args = [block_out, input_grad]
    for spec, (w, g, m, v) in zip(blocks, sets):
        args += [w, g, m, v]
        in_specs += [spec, whole((8, 128)) if g.shape == (8, 128) else spec, spec, spec]
        out_specs += [spec] * 5
        out_shape += [jax.ShapeDtypeStruct(w.shape, F32)] * 4 + [jax.ShapeDtypeStruct(w.shape, BF)]
    return pl.pallas_call(
        finish_kernel, grid=(steps,), out_shape=out_shape, in_specs=in_specs, out_specs=out_specs,
        compiler_params=pltpu.CompilerParams(vmem_limit_bytes=63 * 2**20),
    )(*args)


def per_device(
    tokens, cotangent, group_sizes, prefix_lens, solution_lens,
    w_qkv, w_out, w_up, w_down, norms,
    first_qkv, second_qkv, first_out, second_out,
    first_up, second_up, first_down, second_down, first_norms, second_norms,
):
    block_out, input_grad, grad_qkv, grad_out, grad_up, grad_down, grad_norms = run_layer(
        tokens, cotangent, group_sizes, prefix_lens, solution_lens, norms, w_qkv, w_out, w_up, w_down)
    sets = (
        (w_qkv, grad_qkv, first_qkv, second_qkv),
        (w_out, grad_out, first_out, second_out),
        (w_up, grad_up, first_up, second_up),
        (w_down, grad_down, first_down, second_down),
        (norms, grad_norms, first_norms, second_norms),
    )
    return tuple(finish(block_out, input_grad, sets))


def solution(mesh):
    row, mat = P("dp", None), P("tensor", "dp")
    qkv, up, nrm = P(None, "dp", "tensor"), P("dp", "tensor"), P(None, "dp")
    return jax.shard_map(
        per_device,
        mesh=mesh,
        in_specs=(row, row, P("dp"), P("dp"), row, qkv, mat, up, mat, nrm,
                  qkv, qkv, mat, mat, up, up, mat, mat, nrm, nrm),
        out_specs=(row, row) + (qkv,) * 5 + (mat,) * 5 + (up,) * 5 + (mat,) * 5 + (nrm,) * 5,
        check_vma=False,
    )
```
